128 devices in a mesh: dp: 4 (over z), tensor: 32 (over x, y, core).
Axes of the slice: x: 4, y: 4, z: 4, core: 2. Of those that a mesh axis runs over, the one named last changes fastest.
Arguments:
- tokens: bfloat16 [2048, 8192], P(('dp', 'tensor')), parts along dimension 0, may hold values from -6 to 6
- gate_weight: bfloat16 [8192, 14336], P(None, 'tensor'), may hold values from -0.0625 to 0.0625
- up_weight: bfloat16 [8192, 14336], P(None, 'tensor'), may hold values from -0.0625 to 0.0625
- down_weight: bfloat16 [14336, 8192], P('tensor'), may hold values from -0.046875 to 0.046875
- block_mixing_matrix: bfloat16 [448, 448], replicated, may hold values from -0.25 to 0.25
Outputs:
- mixed: bfloat16 [2048, 8192], P(('dp', 'tensor')), parts along dimension 0
The draws below stay inside these ranges and needn't reach their ends.
There are 4 independent parts, one for each index of `dp`. The reference program is written for one: setup_inputs(seed, part) draws one part's arguments, and reference() takes and returns one part's arrays. A program takes and returns all parts, laid end to end along the dimension named above; an argument that names none is the same for every part. Nothing has to cross between parts.
All inputs are finite; a program needn't handle non-finite values.
Results may differ from the reference program's by a relative error of at most 0.025.
Values may be sent and summed in bfloat16 or wider, within the bound.
No kernel may reach another device: no remote copies, remote signals or barrier semaphores. Data moves between devices by JAX's collectives and lax.ppermute only.
A program may use at most 128 MiB of HBM per device.

```python
import math
import jax
import jax.numpy as jnp
from jax import lax

D = 8192
FF_DEV = 448
TOK = 512
FF = 14336
N_TENSOR = 32


def block_levels(own_key, extent, pieces, least, high):
    def one(axis_at, parts):
        steps = jax.random.uniform(jax.random.fold_in(jax.random.fold_in(own_key, 6), axis_at), (parts,), jnp.float32, least / len(pieces), high / len(pieces))
        return jnp.repeat(jnp.exp(steps), extent[axis_at] // parts).reshape((-1,) + (1,) * (len(extent) - axis_at - 1))

    loudness = one(*pieces[0])
    for cut in pieces[1:]:
        loudness = loudness * one(*cut)
    return loudness


def normal_values(rng, dims, scale, bound, pieces=(), kind=jnp.bfloat16):
    array = scale * jax.random.normal(rng, dims, jnp.float32)
    if pieces:
        array = array * block_levels(rng, dims, pieces, -0.22, 0.18)
    return jnp.clip(array, -bound, bound).astype(kind)


def setup_inputs(seed: int = 0, part: int = 0) -> dict:
    keys = jax.random.split(jax.random.key(seed), 6)
    part_splits = jax.random.split(jax.random.fold_in(keys[5], part), 6)
    tokens = normal_values(part_splits[0], (TOK, D), 1.0, 6.0, ((0, 32),))
    gate_weight = normal_values(keys[1], (D, FF), D ** -0.5, 0.0625, ((1, 32),))
    up_weight = normal_values(keys[2], (D, FF), D ** -0.5, 0.0625, ((1, 32),))
    down_weight = normal_values(keys[3], (FF, D), FF ** -0.5, 0.046875, ((0, 32),))
    block_mixing_matrix = normal_values(keys[4], (FF_DEV, FF_DEV), FF_DEV ** -0.5, 0.25)
    return dict(tokens=tokens, gate_weight=gate_weight, up_weight=up_weight, down_weight=down_weight, block_mixing_matrix=block_mixing_matrix)


def walsh_table(block_members):
    indices = jnp.arange(block_members, dtype=jnp.int32)
    common = jnp.bitwise_and(indices[:, None], indices[None, :])
    parity = jnp.zeros((block_members, block_members), jnp.int32)
    for position in range(block_members.bit_length() - 1):
        parity = jnp.bitwise_xor(parity, jnp.bitwise_and(jnp.right_shift(common, position), 1))
    return (1.0 - 2.0 * parity.astype(jnp.float32)) / math.sqrt(block_members)

def reference(tokens, gate_weight, up_weight, down_weight, block_mixing_matrix):
    gate_part = jnp.dot(tokens, gate_weight, preferred_element_type=jnp.float32)
    up_part = jnp.dot(tokens, up_weight, preferred_element_type=jnp.float32)
    hidden = (jax.nn.silu(gate_part) * up_part).astype(jnp.bfloat16)
    hidden_blocks = hidden.reshape(TOK, N_TENSOR, FF_DEV).astype(jnp.float32)
    local_block_values = jnp.einsum('xqa,ac->xqc', hidden_blocks, block_mixing_matrix.astype(jnp.float32))
    sign_table = walsh_table(N_TENSOR)
    rotated_hidden = jnp.einsum('re,aes->ras', sign_table, local_block_values, precision=lax.Precision.HIGHEST).astype(jnp.bfloat16)
    blocked_weight_rows = down_weight.reshape(N_TENSOR, FF_DEV, D)

    def add_block(total, pair):
        rows, weights = pair
        partial_value = jnp.dot(rows, weights, preferred_element_type=jnp.float32).astype(jnp.bfloat16)
        partial_value = lax.optimization_barrier(partial_value)
        return (total + partial_value.astype(jnp.float32), None)
    total, unused = lax.scan(add_block, jnp.zeros((TOK, D), jnp.float32), (rotated_hidden, blocked_weight_rows))
    return total.astype(jnp.bfloat16)
```

```python
import math

import jax
import jax.numpy as jnp
from jax import lax
from jax.sharding import PartitionSpec as P

RING = 4
PLACES = [(x, y, c) for x in range(RING) for y in range(RING) for c in range(2)]


def place(x, y, c):
    return (x % RING) * RING * 2 + (y % RING) * 2 + c


def along_first(d):
    return [
        (place(x, y, c), place(x + d, y, c) if c == 0 else place(x, y + d, c))
        for x, y, c in PLACES
    ]


def along_second(d):
    return [
        (place(x, y, c), place(x + d, y, c) if c == 1 else place(x, y + d, c))
        for x, y, c in PLACES
    ]


SIBLING = [(place(x, y, c), place(x, y, 1 - c)) for x, y, c in PLACES]


def send(value, pairs):
    return lax.ppermute(value, "tensor", pairs)


def dot(a, b):
    return jnp.dot(a, b, preferred_element_type=jnp.float32)


def sign(row, column):
    common = jnp.bitwise_and(row, column)
    parity = jnp.bitwise_xor(common, jnp.right_shift(common, 1)) & 1
    return 1.0 - 2.0 * parity.astype(jnp.float32)


def rotate(value, along, position, axis, scale):
    came = {0: value, 1: send(value, along(-1)), 2: send(value, along(2)), 3: send(value, along(1))}
    total = 0.0
    for step, part in came.items():
        factor = sign(position, (position + step) % RING) * scale
        total = total + factor * jnp.roll(part, step, axis=axis).astype(jnp.float32)
    return total.astype(jnp.bfloat16)


def body(tokens, gate_weight, up_weight, down_weight, mixing):
    rows, width = tokens.shape
    units = gate_weight.shape[1]
    index = lax.axis_index("tensor")
    core = index % 2
    x, y = index // (2 * RING), (index // 2) % RING
    first = jnp.where(core == 0, x, y)
    second = jnp.where(core == 0, y, x)

    gate_other = send(gate_weight, SIBLING)
    up_other = send(up_weight, SIBLING)
    down_other = send(down_weight, SIBLING)

    chunks = 2
    span = width // chunks
    blocks = []
    for at in range(chunks):
        own = tokens[:, at * span : (at + 1) * span]
        blocks.append(
            jnp.concatenate(
                [own, send(own, along_first(-1)), send(own, along_first(2)), send(own, along_first(1))]
            )
        )
    sums = [0.0] * 4
    for at in range(chunks):
        block = blocks[at]
        ahead = send(block, along_second(-1))
        behind = send(block, along_second(1))
        if at % 2 == 0:
            across = send(behind, along_second(1))
        else:
            across = send(ahead, along_second(-1))
        piece = jnp.concatenate([block, ahead, across, behind])
        part = slice(at * span, (at + 1) * span)
        for n, weight in enumerate((gate_weight, up_weight, gate_other, up_other)):
            sums[n] = sums[n] + dot(piece, weight[part])

    def local(gate, up):
        hidden = (jax.nn.silu(gate) * up).astype(jnp.bfloat16)
        return dot(hidden, mixing)

    local_own = local(sums[0], sums[1])
    local_other = local(sums[2], sums[3])
    turn = 1.0 - 2.0 * core.astype(jnp.float32)
    value = jnp.concatenate(
        [local_other + turn * local_own, local_own - turn * local_other], axis=1
    ).astype(jnp.bfloat16)
    value = value.reshape(RING, RING, rows, 2 * units)
    value = rotate(value, along_first, first, 1, 1.0)
    value = rotate(value, along_second, second, 0, 1.0 / math.sqrt(2 * RING * RING))
    value = value.reshape(RING * RING * rows, 2 * units)

    outs = []
    for at in range(chunks):
        part = slice(at * span, (at + 1) * span)
        partial = dot(value[:, :units], down_weight[:, part]) + dot(
            value[:, units:], down_other[:, part]
        )
        partial = partial.astype(jnp.bfloat16).reshape(RING, RING * rows, span)
        if at % 2 == 0:
            forward, back = 1, 3
        else:
            forward, back = 3, 1
        step = 1 if forward == 1 else -1
        far = send(partial[2], along_second(step))
        near = send(partial[back], along_second(-step))
        onward = (partial[forward].astype(jnp.float32) + far.astype(jnp.float32)).astype(jnp.bfloat16)
        onward = send(onward, along_second(step))
        total = (
            partial[0].astype(jnp.float32) + near.astype(jnp.float32) + onward.astype(jnp.float32)
        )
        total = total.astype(jnp.bfloat16).reshape(RING, rows, span)
        came = [
            send(total[1], along_first(1)),
            send(total[2], along_first(2)),
            send(total[3], along_first(-1)),
        ]
        last = total[0].astype(jnp.float32)
        for part_sum in came:
            last = last + part_sum.astype(jnp.float32)
        outs.append(last.astype(jnp.bfloat16))
    return jnp.concatenate(outs, axis=1)


def solution(mesh):
    in_specs = (
        P(("dp", "tensor"), None),
        P(None, "tensor"),
        P(None, "tensor"),
        P("tensor", None),
        P(),
    )
    out_specs = P(("dp", "tensor"), None)
    return jax.shard_map(body, mesh=mesh, in_specs=in_specs, out_specs=out_specs, check_vma=False)
```

```python
import functools
import math

import jax
import jax.numpy as jnp
import numpy as np
from jax import lax
from jax.experimental import pallas as pl
from jax.experimental.pallas import tpu as pltpu
from jax.sharding import PartitionSpec as P

RING = 4
PLACES = [(x, y, c) for x in range(RING) for y in range(RING) for c in range(2)]
GATHER_SPANS = (3072, 3072, 2048)
OUT_SPANS = (4096, 4096)
LIMIT = 40 * 2**20
BY_ROWS = (((1,), (1,)), ((), ()))


def place(x, y, c):
    return (x % RING) * RING * 2 + (y % RING) * 2 + c


def along_first(d):
    return [
        (place(x, y, c), place(x + d, y, c) if c == 0 else place(x, y + d, c))
        for x, y, c in PLACES
    ]


def along_second(d):
    return [
        (place(x, y, c), place(x + d, y, c) if c == 1 else place(x, y + d, c))
        for x, y, c in PLACES
    ]


SIBLING = [(place(x, y, c), place(x, y, 1 - c)) for x, y, c in PLACES]


def send(value, pairs):
    return lax.ppermute(value, "tensor", pairs)


def from_steps(value, along):
    return send(value, along(-1)), send(value, along(2)), send(value, along(1))


def dot(a, b):
    return jnp.dot(a, b, preferred_element_type=jnp.float32)


def scalar_table():
    def sign(row, column):
        return 1.0 - 2.0 * (bin(row & column).count("1") % 2)

    rows = []
    for x, y, c in PLACES:
        first, second = (x, y) if c == 0 else (y, x)
        row = [1.0 - 2.0 * c]
        row += [sign(first, (first + s) % RING) for s in range(RING)]
        row += [
            sign(second, (second + s) % RING) / math.sqrt(2 * RING * RING) for s in range(RING)
        ]
        rows.append(row + [0.0] * (16 - len(row)))
    return np.array(rows, np.float32)


def spans(widths, total):
    cut = [w * total // sum(widths) for w in widths]
    starts = [sum(cut[:n]) for n in range(len(cut))]
    return list(zip(starts, cut))


def step_of(span):
    for size in (2048, 1536, 1024, 512, 256, 128):
        if span % size == 0 and span // size >= 2:
            return size
    return span


def call(kernel, name, flops, size, **kwargs):
    return pl.pallas_call(
        kernel,
        name=name,
        compiler_params=pltpu.CompilerParams(vmem_limit_bytes=LIMIT),
        cost_estimate=pl.CostEstimate(flops=flops, bytes_accessed=size, transcendentals=0),
        **kwargs,
    )


SCALARS = pl.BlockSpec(memory_space=pltpu.SMEM)


def gate_up(pieces, weights, at, span, sums, finish):
    rows = RING * pieces[0].shape[0]
    units = weights[0].shape[0]
    block = step_of(span)
    steps = span // block
    offset = at // block
    opening, closing = sums is None, finish is not None

    def kernel(*refs):
        refs = list(refs)
        parts, loads = refs[:4], refs[4:8]
        refs = refs[8:]
        before = None if opening else refs.pop(0)
        if closing:
            mixing, scalars, out, held = refs
        else:
            (held,) = refs
        step = pl.program_id(0)
        x = jnp.concatenate([part[...] for part in parts], axis=0)
        for n, load in enumerate(loads):
            product = lax.dot_general(x, load[...], BY_ROWS, preferred_element_type=jnp.float32)

            @pl.when(step == 0)
            def _():
                held[n] = product if opening else before[n] + product

            @pl.when(step > 0)
            def _():
                held[n] = held[n] + product

        if closing:

            @pl.when(step == steps - 1)
            def _():
                local = []
                for n in (0, 2):
                    gate, up = held[n], held[n + 1]
                    hidden = (gate / (1.0 + jnp.exp(-gate)) * up).astype(jnp.bfloat16)
                    local.append(dot(hidden, mixing[...]))
                own, other = local
                turn = scalars[0]
                out[:, :units] = (other + turn * own).astype(jnp.bfloat16)
                out[:, units:] = (own - turn * other).astype(jnp.bfloat16)

    whole = (4, rows, units)
    in_specs = [pl.BlockSpec((rows // RING, block), lambda k: (0, k))] * 4
    in_specs += [pl.BlockSpec((units, block), lambda k: (0, k + offset))] * 4
    operands = [*pieces, *weights]
    if not opening:
        in_specs.append(pl.BlockSpec(whole, lambda k: (0, 0, 0)))
        operands.append(sums)
    if closing:
        mixing, scalars = finish
        in_specs += [pl.BlockSpec(mixing.shape, lambda k: (0, 0)), SCALARS]
        operands += [mixing, scalars]
        extra = dict(
            out_shape=jax.ShapeDtypeStruct((rows, 2 * units), jnp.bfloat16),
            out_specs=pl.BlockSpec((rows, 2 * units), lambda k: (0, 0)),
            scratch_shapes=[pltpu.VMEM(whole, jnp.float32)],
        )
    else:
        extra = dict(
            out_shape=jax.ShapeDtypeStruct(whole, jnp.float32),
            out_specs=pl.BlockSpec(whole, lambda k: (0, 0, 0)),
            input_output_aliases={} if opening else {8: 0},
        )
    return call(
        kernel,
        "gate_up",
        8 * rows * units * span,
        8 * units * span + 2 * rows * span,
        grid=(steps,),
        in_specs=in_specs,
        **extra,
    )(*operands)


def combine(parts, scalars, first_scalar, major):
    rows, width = parts[0].shape
    slot = rows // (RING * RING)

    def kernel(own, one, two, three, factors, out):
        came = (own, one, two, three)
        for i in range(RING):
            for j in range(RING):
                total = 0.0
                for s in range(RING):
                    where = ((i - s) % RING, j) if major else (i, (j - s) % RING)
                    at = (where[0] * RING + where[1]) * slot
                    total = total + factors[first_scalar + s] * came[s][at : at + slot].astype(
                        jnp.float32
                    )
                at = (i * RING + j) * slot
                out[at : at + slot] = total.astype(jnp.bfloat16)

    return call(
        kernel,
        "combine",
        0,
        10 * rows * width,
        in_specs=[pl.BlockSpec(memory_space=pltpu.VMEM)] * 4 + [SCALARS],
        out_specs=pl.BlockSpec(memory_space=pltpu.VMEM),
        out_shape=jax.ShapeDtypeStruct((rows, width), jnp.bfloat16),
    )(*parts, scalars)


def down(value, weight, other, at, span):
    rows = value.shape[0]
    units = weight.shape[0]
    block = step_of(span)
    offset = at // block

    def kernel(held, load, load_other, *outs):
        product = dot(held[:, :units], load[...]) + dot(held[:, units:], load_other[...])
        product = product.astype(jnp.bfloat16)
        for n, out in enumerate(outs):
            out[...] = product[n * (rows // RING) : (n + 1) * (rows // RING)]

    return call(
        kernel,
        "down",
        4 * rows * units * span,
        4 * units * span + 2 * rows * span,
        grid=(span // block,),
        in_specs=[pl.BlockSpec(value.shape, lambda k: (0, 0))]
        + [pl.BlockSpec((units, block), lambda k: (0, k + offset))] * 2,
        out_specs=[pl.BlockSpec((rows // RING, block), lambda k: (0, k))] * RING,
        out_shape=[jax.ShapeDtypeStruct((rows // RING, span), jnp.bfloat16)] * RING,
    )(value, weight, other)


def fold(own, near, onward):
    rows, width = own.shape

    def kernel(own, near, onward, *outs):
        for n, out in enumerate(outs):
            at = slice(n * (rows // RING), (n + 1) * (rows // RING))
            total = (
                own[at].astype(jnp.float32)
                + near[at].astype(jnp.float32)
                + onward[at].astype(jnp.float32)
            )
            out[...] = total.astype(jnp.bfloat16)

    return call(
        kernel,
        "fold",
        0,
        8 * rows * width,
        in_specs=[pl.BlockSpec(memory_space=pltpu.VMEM)] * 3,
        out_specs=[pl.BlockSpec(memory_space=pltpu.VMEM)] * RING,
        out_shape=[jax.ShapeDtypeStruct((rows // RING, width), jnp.bfloat16)] * RING,
    )(own, near, onward)


def body(tokens, gate_weight, up_weight, down_weight, mixing):
    width = tokens.shape[1]
    index = lax.axis_index("tensor")
    scalars = lax.dynamic_index_in_dim(jnp.asarray(scalar_table()), index, keepdims=False)

    gate, up = gate_weight.T, up_weight.T
    near = from_steps(tokens, along_first)
    weights = [gate, up, send(gate, SIBLING), send(up, SIBLING)]
    down_other = send(down_weight, SIBLING)

    sums = None
    cuts = spans(GATHER_SPANS, width)
    for n, (at, span) in enumerate(cuts):
        part = slice(at, at + span)
        block = jnp.concatenate([tokens[:, part]] + [piece[:, part] for piece in near])
        ahead, across, behind = from_steps(block, along_second)
        finish = (mixing, scalars) if n == len(cuts) - 1 else None
        sums = gate_up((block, ahead, across, behind), weights, at, span, sums, finish)

    value = sums
    value = combine((value, *from_steps(value, along_first)), scalars, 1, False)
    value = combine((value, *from_steps(value, along_second)), scalars, 1 + RING, True)

    came = []
    for n, (at, span) in enumerate(spans(OUT_SPANS, width)):
        parts = down(value, down_weight, down_other, at, span)
        forward, back, step = (1, 3, 1) if n % 2 == 0 else (3, 1, -1)
        far = send(parts[2], along_second(step))
        near = send(parts[back], along_second(-step))
        onward = (parts[forward].astype(jnp.float32) + far.astype(jnp.float32)).astype(jnp.bfloat16)
        onward = send(onward, along_second(step))
        total = fold(parts[0], near, onward)
        came.append(
            [
                total[0],
                send(total[1], along_first(1)),
                send(total[2], along_first(2)),
                send(total[3], along_first(-1)),
            ]
        )
    outs = []
    for parts in came:
        outs.append(sum(part.astype(jnp.float32) for part in parts).astype(jnp.bfloat16))
    return jnp.concatenate(outs, axis=1)


def solution(mesh):
    in_specs = (
        P(("dp", "tensor"), None),
        P(None, "tensor"),
        P(None, "tensor"),
        P("tensor", None),
        P(),
    )
    out_specs = P(("dp", "tensor"), None)
    return jax.shard_map(body, mesh=mesh, in_specs=in_specs, out_specs=out_specs, check_vma=False)
```

```python
import math

import jax
import jax.numpy as jnp
import numpy as np
from jax import lax
from jax.experimental import pallas as pl
from jax.experimental.pallas import tpu as pltpu
from jax.sharding import PartitionSpec as P

RING = 4
PLACES = [(x, y, c) for x in range(RING) for y in range(RING) for c in range(2)]
GATHER_SPANS = (3, 3, 2)
LIMIT = 14 * 2**20
BY_ROWS = (((1,), (1,)), ((), ()))


def place(x, y, c):
    return (x % RING) * RING * 2 + (y % RING) * 2 + c


def along_first(d):
    return [
        (place(x, y, c), place(x + d, y, c) if c == 0 else place(x, y + d, c))
        for x, y, c in PLACES
    ]


def along_second(d):
    return [
        (place(x, y, c), place(x + d, y, c) if c == 1 else place(x, y + d, c))
        for x, y, c in PLACES
    ]


PAIRS = [[place(x, y, 0), place(x, y, 1)] for x in range(RING) for y in range(RING)]
SIBLING = [(place(x, y, c), place(x, y, 1 - c)) for x, y, c in PLACES]


def send(value, pairs):
    return lax.ppermute(value, "tensor", pairs)


def from_steps(value, along):
    return send(value, along(-1)), send(value, along(2)), send(value, along(1))


def after(value, *others):
    return lax.optimization_barrier((value, *others))[0]


def dot(a, b):
    return jnp.dot(a, b, preferred_element_type=jnp.float32)


def scalar_table():
    def sign(row, column):
        return 1.0 - 2.0 * (bin(row & column).count("1") % 2)

    rows = []
    for x, y, c in PLACES:
        first, second = (x, y) if c == 0 else (y, x)
        row = [1.0 - 2.0 * c]
        row += [sign(first, (first + s) % RING) for s in range(RING)]
        row += [
            sign(second, (second + s) % RING) / math.sqrt(2 * RING * RING) for s in range(RING)
        ]
        rows.append(row + [0.0] * (16 - len(row)))
    return np.array(rows, np.float32)


def cuts_of(shares, total):
    widths = [w * total // sum(shares) for w in shares]
    starts = [sum(widths[:n]) for n in range(len(widths))]
    return list(zip(starts, widths))


VMEM = pl.BlockSpec(memory_space=pltpu.VMEM)
SCALARS = pl.BlockSpec(memory_space=pltpu.SMEM)


def call(kernel, name, flops, size, operands, outs, specs=None, **kwargs):
    return pl.pallas_call(
        kernel,
        name=name,
        compiler_params=pltpu.CompilerParams(vmem_limit_bytes=LIMIT),
        cost_estimate=pl.CostEstimate(flops=flops, bytes_accessed=size, transcendentals=0),
        in_specs=specs or [VMEM] * len(operands),
        out_specs=[VMEM] * len(outs),
        out_shape=outs,
        **kwargs,
    )(*operands)


def load(first, second, at, span, rows, skip):
    def kernel(first, second, first_out, second_out, sems):
        columns = pl.ds(at, span)
        copies = [
            pltpu.make_async_copy(first.at[:rows, columns], first_out, sems.at[0]),
            pltpu.make_async_copy(second.at[skip : skip + rows, columns], second_out, sems.at[1]),
        ]
        for copy in copies:
            copy.start()
        for copy in copies:
            copy.wait()

    return pl.pallas_call(
        kernel,
        name="load",
        compiler_params=pltpu.CompilerParams(vmem_limit_bytes=LIMIT),
        cost_estimate=pl.CostEstimate(flops=0, bytes_accessed=4 * rows * span, transcendentals=0),
        in_specs=[pl.BlockSpec(memory_space=pltpu.HBM)] * 2,
        out_specs=[VMEM] * 2,
        out_shape=[pltpu.VMEM((rows, span), first.dtype)] * 2,
        scratch_shapes=[pltpu.SemaphoreType.DMA((2,))],
    )(
        pltpu.with_memory_space_constraint(first, pltpu.HBM),
        pltpu.with_memory_space_constraint(second, pltpu.HBM),
    )


def gate_up(pieces, weights, at, span, sums, mixing, streamed):
    rows = RING * pieces[0].shape[0]
    units = weights[0].shape[0]
    block = math.gcd(span, 1024) if streamed else span
    steps = span // block
    opening, closing = sums is None, mixing is not None

    def kernel(*refs):
        refs = list(refs)
        held = refs.pop()
        parts, loads, refs = refs[:RING], refs[RING : RING + 2], refs[RING + 2 :]
        before = None if opening else refs.pop(0)
        mix = refs.pop(0) if closing else None
        (out,) = refs
        total = held if closing else out
        step = pl.program_id(0)
        x = jnp.concatenate([part[...] for part in parts], axis=0)
        for m in range(2):
            product = lax.dot_general(
                x, loads[m][...], BY_ROWS, preferred_element_type=jnp.float32
            )

            @pl.when(step == 0)
            def _():
                total[m] = product if opening else before[m] + product

            @pl.when(step > 0)
            def _():
                total[m] = total[m] + product

        if closing:

            @pl.when(step == steps - 1)
            def _():
                gate, up = total[0], total[1]
                hidden = (gate / (1.0 + jnp.exp(-gate)) * up).astype(jnp.bfloat16)
                out[...] = dot(hidden, mix[...]).astype(jnp.bfloat16)

    operands = [*pieces, *weights]
    if streamed:
        specs = [pl.BlockSpec((rows // RING, block), lambda k: (0, k))] * RING
        specs += [pl.BlockSpec((units, block), lambda k: (0, k + at // block))] * 2
    else:
        specs = [VMEM] * (RING + 2)
    if not opening:
        operands.append(sums)
        specs.append(VMEM)
    if closing:
        operands.append(mixing)
        specs.append(VMEM)
        out = jax.ShapeDtypeStruct((rows, units), jnp.bfloat16)
    else:
        out = jax.ShapeDtypeStruct((2, rows, units), jnp.float32)
    return call(
        kernel,
        "gate_up",
        4 * rows * units * span,
        4 * units * span,
        operands,
        [out],
        specs,
        grid=(steps,),
        scratch_shapes=[pltpu.VMEM((2, rows, units), jnp.float32)],
    )[0]


def turned(came, factors, first_scalar, i, j, major, slot):
    total = 0.0
    for s in range(RING):
        where = ((i - s) % RING, j) if major else (i, (j - s) % RING)
        at = (where[0] * RING + where[1]) * slot
        total = total + factors[first_scalar + s] * came[s][at : at + slot].astype(jnp.float32)
    return total


def first_ring(parts, scalars):
    rows, width = parts[0].shape
    slot = rows // (RING * RING)

    def kernel(own, one, two, three, factors, out):
        for i in range(RING):
            for j in range(RING):
                at = (i * RING + j) * slot
                out[at : at + slot] = turned(
                    (own, one, two, three), factors, 1, i, j, False, slot
                ).astype(jnp.bfloat16)

    return call(
        kernel,
        "first_ring",
        0,
        10 * rows * width,
        [*parts, scalars],
        [jax.ShapeDtypeStruct((rows, width), jnp.bfloat16)],
        [VMEM] * 4 + [SCALARS],
    )[0]


def second_ring(own_parts, other_parts, scalars):
    rows, width = own_parts[0].shape
    slot = rows // (RING * RING)

    def kernel(*refs):
        factors, sum_out, difference_out = refs[8:]
        turn = factors[0]
        for i in range(RING):
            for j in range(RING):
                at = (i * RING + j) * slot
                own = turned(refs[:4], factors, 1 + RING, i, j, True, slot)
                other = turned(refs[4:8], factors, 1 + RING, i, j, True, slot)
                sum_out[at : at + slot] = (own + other).astype(jnp.bfloat16)
                difference_out[at : at + slot] = (turn * (own - other)).astype(jnp.bfloat16)

    return call(
        kernel,
        "second_ring",
        0,
        20 * rows * width,
        [*own_parts, *other_parts, scalars],
        [jax.ShapeDtypeStruct((rows, width), jnp.bfloat16)] * 2,
        [VMEM] * 8 + [SCALARS],
    )


def down(values, weights, span):
    rows, units = values[0].shape
    group = rows // RING
    block = min(span, 512)

    def kernel(zero, one, loaded, loaded_one, *outs):
        for start in range(0, span, block):
            where = slice(start, start + block)
            product = dot(zero[...], loaded[:, where]) + dot(one[...], loaded_one[:, where])
            product = product.astype(jnp.bfloat16)
            for n, out in enumerate(outs):
                out[:, where] = product[n * group : (n + 1) * group]

    return call(
        kernel,
        "down",
        4 * rows * units * span,
        4 * units * span,
        [*values, *weights],
        [jax.ShapeDtypeStruct((group, span), jnp.bfloat16)] * RING,
    )


def added(a, b):
    return (a.astype(jnp.float32) + b.astype(jnp.float32)).astype(jnp.bfloat16)


def fold(thirds):
    group = thirds[0][0].shape[0]
    rows = group // RING
    width = sum(parts[0].shape[1] for parts in thirds)

    def kernel(*refs):
        ins, outs = refs[: 3 * len(thirds)], refs[3 * len(thirds) :]
        start = 0
        for n in range(len(thirds)):
            parts = ins[3 * n : 3 * n + 3]
            stop = start + parts[0].shape[1]
            for m, out in enumerate(outs):
                at = slice(m * rows, (m + 1) * rows)
                total = sum(part[at].astype(jnp.float32) for part in parts)
                out[:, start:stop] = total.astype(jnp.bfloat16)
            start = stop

    return call(
        kernel,
        "fold",
        0,
        8 * group * width,
        [part for parts in thirds for part in parts],
        [jax.ShapeDtypeStruct((rows, width), jnp.bfloat16)] * RING,
    )


def body(tokens, gate_weight, up_weight, down_weight, mixing):
    width = tokens.shape[1]
    index = lax.axis_index("tensor")
    scalars = lax.dynamic_index_in_dim(jnp.asarray(scalar_table()), index, keepdims=False)

    gate, up = gate_weight.T, up_weight.T
    near = from_steps(tokens, along_first)
    gate_other = send(gate, SIBLING)
    up_other = send(up, SIBLING)
    both_down = lax.all_gather(down_weight, "tensor", axis=0, tiled=True, axis_index_groups=PAIRS)
    cuts = cuts_of(GATHER_SPANS, width)
    units = gate.shape[0]
    own_weights = [load(gate, up, *cut, units, 0) for cut in cuts]
    tokens = after(tokens, *own_weights[0])

    own = other = None
    for n, (at, span) in enumerate(cuts):
        part = slice(at, at + span)
        block = jnp.concatenate([tokens[:, part]] + [piece[:, part] for piece in near])
        ahead, behind = send(block, along_second(-1)), send(block, along_second(1))
        if n == 0:
            across = send(behind, along_second(1))
        elif n == 1:
            across = send(ahead, along_second(-1))
        else:
            across = send(block, along_second(2))
        pieces = (block, ahead, across, behind)
        mix = mixing if n == len(cuts) - 1 else None
        own = gate_up(pieces, own_weights[n], at, span, own, mix, False)
        other = gate_up(pieces, (gate_other, up_other), at, span, other, mix, True)

    own = first_ring((own, *from_steps(own, along_first)), scalars)
    other = first_ring((other, *from_steps(other, along_first)), scalars)
    both = second_ring(
        (own, *from_steps(own, along_second)), (other, *from_steps(other, along_second)), scalars
    )

    half = width // 2
    halves = (both_down, both_down)
    left = down(both, load(*halves, 0, half, units, units), half)
    right = down(both, load(*halves, half, half, units, units), half)
    left_far = send(left[2], along_second(1))
    right_far = send(right[2], along_second(-1))
    right_near = send(right[1], along_second(1))
    left_near = send(left[3], along_second(-1))
    left_on = send(added(left[1], left_far), along_second(1))
    right_on = send(added(right[3], right_far), along_second(-1))
    parts = fold([(left[0], left_near, left_on), (right[0], right_near, right_on)])
    came = [
        parts[0],
        send(parts[1], along_first(1)),
        send(parts[2], along_first(2)),
        send(parts[3], along_first(-1)),
    ]
    return sum(part.astype(jnp.float32) for part in came).astype(jnp.bfloat16)


def solution(mesh):
    in_specs = (
        P(("dp", "tensor"), None),
        P(None, "tensor"),
        P(None, "tensor"),
        P("tensor", None),
        P(),
    )
    out_specs = P(("dp", "tensor"), None)
    return jax.shard_map(body, mesh=mesh, in_specs=in_specs, out_specs=out_specs, check_vma=False)
```

```python
import math

import jax
import jax.numpy as jnp
import numpy as np
from jax import lax
from jax.experimental import pallas as pl
from jax.experimental.pallas import tpu as pltpu
from jax.sharding import PartitionSpec as P

RING = 4
PLACES = [(x, y, c) for x in range(RING) for y in range(RING) for c in range(2)]
GATHER_SPANS = (3, 3, 2)
LIMIT = 24 * 2**20
BY_ROWS = (((1,), (1,)), ((), ()))


def place(x, y, c):
    return (x % RING) * RING * 2 + (y % RING) * 2 + c


def along_first(d):
    return [
        (place(x, y, c), place(x + d, y, c) if c == 0 else place(x, y + d, c))
        for x, y, c in PLACES
    ]


def along_second(d):
    return [
        (place(x, y, c), place(x + d, y, c) if c == 1 else place(x, y + d, c))
        for x, y, c in PLACES
    ]


SIBLING = [(place(x, y, c), place(x, y, 1 - c)) for x, y, c in PLACES]


def send(value, pairs):
    return lax.ppermute(value, "tensor", pairs)


def from_steps(value, along):
    return send(value, along(-1)), send(value, along(2)), send(value, along(1))


def after(value, *others):
    return lax.optimization_barrier((value, *others))[0]


def dot(a, b):
    return jnp.dot(a, b, preferred_element_type=jnp.float32)


def scalar_table():
    def sign(row, column):
        return 1.0 - 2.0 * (bin(row & column).count("1") % 2)

    rows = []
    for x, y, c in PLACES:
        first, second = (x, y) if c == 0 else (y, x)
        row = [1.0 - 2.0 * c]
        row += [sign(first, (first + s) % RING) for s in range(RING)]
        row += [
            sign(second, (second + s) % RING) / math.sqrt(2 * RING * RING) for s in range(RING)
        ]
        rows.append(row + [0.0] * (16 - len(row)))
    return np.array(rows, np.float32)


def cuts_of(shares, total):
    widths = [w * total // sum(shares) for w in shares]
    starts = [sum(widths[:n]) for n in range(len(widths))]
    return list(zip(starts, widths))


VMEM = pl.BlockSpec(memory_space=pltpu.VMEM)
SCALARS = pl.BlockSpec(memory_space=pltpu.SMEM)


def call(kernel, name, flops, size, operands, outs, specs=None, **kwargs):
    return pl.pallas_call(
        kernel,
        name=name,
        compiler_params=pltpu.CompilerParams(vmem_limit_bytes=LIMIT),
        cost_estimate=pl.CostEstimate(flops=flops, bytes_accessed=size, transcendentals=0),
        in_specs=specs or [VMEM] * len(operands),
        out_specs=[VMEM] * len(outs),
        out_shape=outs,
        **kwargs,
    )(*operands)


def in_hbm(value):
    return pltpu.with_memory_space_constraint(value, pltpu.HBM)


def load(value):
    def kernel(value, out, sem):
        copy = pltpu.make_async_copy(value, out, sem)
        copy.start()
        copy.wait()

    return pl.pallas_call(
        kernel,
        name="load",
        compiler_params=pltpu.CompilerParams(vmem_limit_bytes=LIMIT),
        cost_estimate=pl.CostEstimate(
            flops=0, bytes_accessed=2 * value.size, transcendentals=0
        ),
        in_specs=[pl.BlockSpec(memory_space=pltpu.HBM)],
        out_specs=VMEM,
        out_shape=pltpu.VMEM(value.shape, value.dtype),
        scratch_shapes=[pltpu.SemaphoreType.DMA],
    )(in_hbm(value))


def stack(parts, cuts):
    rows = parts[0].shape[0]

    def kernel(*refs):
        ins, outs = refs[: len(parts)], refs[len(parts) :]
        for (at, span), out in zip(cuts, outs):
            for n, part in enumerate(ins):
                out[n * rows : (n + 1) * rows] = part[:, at : at + span]

    return call(
        kernel,
        "stack",
        0,
        sum(4 * rows * len(parts) * span for _, span in cuts),
        parts,
        [jax.ShapeDtypeStruct((rows * len(parts), span), jnp.bfloat16) for _, span in cuts],
    )


def gate_up(tokens, weights, at, span, sums, mixing):
    rows = tokens[0].shape[0]
    units = weights[0].shape[0]
    block = math.gcd(span, 1024)
    steps = span // block
    count = len(tokens)
    opening, closing = sums is None, mixing is not None

    def kernel(*refs):
        refs = list(refs)
        parts, loads, refs = refs[:count], refs[count : count + 2], refs[count + 2 :]
        before, refs = (None, refs) if opening else (refs[:count], refs[count:])
        mix = refs.pop(0) if closing else None
        outs, totals = refs[:count], refs[count:] if closing else refs[:count]
        step = pl.program_id(0)

        @pl.when(step == 0)
        def _():
            for n, total in enumerate(totals):
                total[...] = jnp.zeros(total.shape, total.dtype) if opening else before[n][...]

        for part, total in zip(parts, totals):
            for m in range(2):
                total[m] += lax.dot_general(
                    part[...], loads[m][...], BY_ROWS, preferred_element_type=jnp.float32
                )

        if closing:

            @pl.when(step == steps - 1)
            def _():
                for total, out in zip(totals, outs):
                    gate, up = total[0], total[1]
                    hidden = (gate / (1.0 + jnp.exp(-gate)) * up).astype(jnp.bfloat16)
                    out[...] = dot(hidden, mix[...]).astype(jnp.bfloat16)

    operands = [*tokens, *[in_hbm(w) for w in weights]]
    specs = [pl.BlockSpec((rows, block), lambda k: (0, k))] * count
    specs += [pl.BlockSpec((units, block), lambda k: (0, k + at // block))] * 2
    if not opening:
        operands += sums
        specs += [VMEM] * count
    kwargs = {}
    if closing:
        operands.append(mixing)
        specs.append(VMEM)
        outs = [jax.ShapeDtypeStruct((rows, units), jnp.bfloat16)] * count
        kwargs["scratch_shapes"] = [pltpu.VMEM((2, rows, units), jnp.float32)] * count
    else:
        outs = [jax.ShapeDtypeStruct((2, rows, units), jnp.float32)] * count
    return call(
        kernel,
        "gate_up",
        4 * count * rows * units * span,
        4 * units * span,
        operands,
        outs,
        specs,
        grid=(steps,),
        **kwargs,
    )


def turned(came, factors, first_scalar, i, j, major, slot):
    total = 0.0
    for s in range(RING):
        where = ((i - s) % RING, j) if major else (i, (j - s) % RING)
        at = (where[0] * RING + where[1]) * slot
        total = total + factors[first_scalar + s] * came[s][at : at + slot].astype(jnp.float32)
    return total


def first_ring(parts, scalars):
    rows, width = parts[0].shape
    slot = rows // (RING * RING)

    def kernel(own, one, two, three, factors, out):
        for i in range(RING):
            for j in range(RING):
                at = (i * RING + j) * slot
                out[at : at + slot] = turned(
                    (own, one, two, three), factors, 1, i, j, False, slot
                ).astype(jnp.bfloat16)

    return call(
        kernel,
        "first_ring",
        0,
        10 * rows * width,
        [*parts, scalars],
        [jax.ShapeDtypeStruct((rows, width), jnp.bfloat16)],
        [VMEM] * 4 + [SCALARS],
    )[0]


def second_ring(own_parts, other_parts, scalars):
    rows, width = own_parts[0].shape
    slot = rows // (RING * RING)

    def kernel(*refs):
        factors, own_out, other_out = refs[8:]
        turn = factors[0]
        for i in range(RING):
            for j in range(RING):
                at = (i * RING + j) * slot
                own = turned(refs[:4], factors, 1 + RING, i, j, True, slot)
                other = turned(refs[4:8], factors, 1 + RING, i, j, True, slot)
                own_out[at : at + slot] = (other + turn * own).astype(jnp.bfloat16)
                other_out[at : at + slot] = (own - turn * other).astype(jnp.bfloat16)

    return call(
        kernel,
        "second_ring",
        0,
        20 * rows * width,
        [*own_parts, *other_parts, scalars],
        [jax.ShapeDtypeStruct((rows, width), jnp.bfloat16)] * 2,
        [VMEM] * 8 + [SCALARS],
    )


def down(values, weights, at, span):
    rows, units = values[0].shape
    group = rows // RING
    block = min(span, 512)

    def kernel(held, held_other, loaded, loaded_other, *outs):
        for start in range(0, span, block):
            where = slice(at + start, at + start + block)
            product = dot(held[...], loaded[:, where]) + dot(
                held_other[...], loaded_other[:, where]
            )
            product = product.astype(jnp.bfloat16)
            for n, out in enumerate(outs):
                out[:, start : start + block] = product[n * group : (n + 1) * group]

    return call(
        kernel,
        "down",
        4 * rows * units * span,
        4 * units * span,
        [*values, *weights],
        [jax.ShapeDtypeStruct((group, span), jnp.bfloat16)] * RING,
    )


def fold(sides):
    count = len(sides[0])
    group = sides[0][0].shape[0]
    rows = group // RING
    width = sum(parts[0].shape[1] for parts in sides)

    def kernel(*refs):
        ins, outs = refs[: count * len(sides)], refs[count * len(sides) :]
        start = 0
        for n in range(len(sides)):
            parts = ins[count * n : count * (n + 1)]
            stop = start + parts[0].shape[1]
            for m, out in enumerate(outs):
                at = slice(m * rows, (m + 1) * rows)
                total = sum(part[at].astype(jnp.float32) for part in parts)
                out[:, start:stop] = total.astype(jnp.bfloat16)
            start = stop

    return call(
        kernel,
        "fold",
        0,
        10 * group * width,
        [part for parts in sides for part in parts],
        [jax.ShapeDtypeStruct((rows, width), jnp.bfloat16)] * RING,
    )


def to_steps(parts, along):
    return parts[0], send(parts[1], along(1)), send(parts[2], along(2)), send(parts[3], along(-1))


def body(tokens, gate_weight, up_weight, down_weight, mixing):
    width = tokens.shape[1]
    index = lax.axis_index("tensor")
    scalars = lax.dynamic_index_in_dim(jnp.asarray(scalar_table()), index, keepdims=False)

    weights = (gate_weight.T, up_weight.T)
    down_other = send(down_weight, SIBLING)

    cuts = cuts_of(GATHER_SPANS, width)
    blocks = stack((tokens, *from_steps(tokens, along_first)), cuts)
    sums, held = None, None
    for n, (at, span) in enumerate(cuts):
        parts = (blocks[n], *from_steps(blocks[n], along_second))
        if n == 2:
            parts = after(parts, sums)
        (mine,) = stack(parts, [(0, span)])
        if n == 0:
            mine = after(mine, down_other)
        theirs = send(mine, SIBLING)
        if n > 0:
            sums = gate_up(held, weights, *cuts[n - 1], sums, None)
        held = (mine, theirs)
    (own,) = gate_up((mine,), weights, at, span, sums[:1], mixing)
    (other,) = gate_up((after(theirs, own),), weights, at, span, sums[1:], mixing)
    other = send(other, SIBLING)

    own = first_ring((own, *from_steps(own, along_first)), scalars)
    other = first_ring((other, *from_steps(other, along_first)), scalars)
    loaded = (load(down_weight), pltpu.with_memory_space_constraint(down_other, pltpu.VMEM))
    own = after(own, loaded[0])
    both = second_ring(
        (own, *from_steps(own, along_second)), (other, *from_steps(other, along_second)), scalars
    )
    half = width // 2
    sides = [to_steps(down(both, loaded, at, half), along_second) for at in (0, half)]
    parts = to_steps(fold(sides), along_first)
    return sum(part.astype(jnp.float32) for part in parts).astype(jnp.bfloat16)


def solution(mesh):
    in_specs = (
        P(("dp", "tensor"), None),
        P(None, "tensor"),
        P(None, "tensor"),
        P("tensor", None),
        P(),
    )
    out_specs = P(("dp", "tensor"), None)
    return jax.shard_map(body, mesh=mesh, in_specs=in_specs, out_specs=out_specs, check_vma=False)
```

```python
import math

import jax
import jax.numpy as jnp
import numpy as np
from jax import lax
from jax.experimental import pallas as pl
from jax.experimental.pallas import tpu as pltpu
from jax.sharding import PartitionSpec as P

RING = 4
PLACES = [(x, y, c) for x in range(RING) for y in range(RING) for c in range(2)]
GATHER_SPANS = (1, 1)
LIMIT = 40 * 2**20
BY_ROWS = (((1,), (1,)), ((), ()))


def place(x, y, c):
    return (x % RING) * RING * 2 + (y % RING) * 2 + c


def along_first(d):
    return [
        (place(x, y, c), place(x + d, y, c) if c == 0 else place(x, y + d, c))
        for x, y, c in PLACES
    ]


def along_second(d):
    return [
        (place(x, y, c), place(x + d, y, c) if c == 1 else place(x, y + d, c))
        for x, y, c in PLACES
    ]


SIBLING = [(place(x, y, c), place(x, y, 1 - c)) for x, y, c in PLACES]


def send(value, pairs):
    return lax.ppermute(value, "tensor", pairs)


def from_steps(value, along):
    return send(value, along(-1)), send(value, along(2)), send(value, along(1))


def after(value, *others):
    return lax.optimization_barrier((value, *others))[0]


def dot(a, b):
    return jnp.dot(a, b, preferred_element_type=jnp.float32)


def scalar_table():
    def sign(row, column):
        return 1.0 - 2.0 * (bin(row & column).count("1") % 2)

    rows = []
    for x, y, c in PLACES:
        first, second = (x, y) if c == 0 else (y, x)
        row = [1.0 - 2.0 * c]
        row += [sign(first, (first + s) % RING) for s in range(RING)]
        row += [
            sign(second, (second + s) % RING) / math.sqrt(2 * RING * RING) for s in range(RING)
        ]
        rows.append(row + [0.0] * (16 - len(row)))
    return np.array(rows, np.float32)


def cuts_of(shares, total):
    widths = [w * total // sum(shares) for w in shares]
    starts = [sum(widths[:n]) for n in range(len(widths))]
    return list(zip(starts, widths))


VMEM = pl.BlockSpec(memory_space=pltpu.VMEM)
SCALARS = pl.BlockSpec(memory_space=pltpu.SMEM)


def call(kernel, name, flops, size, operands, outs, specs=None, out_specs=None, **kwargs):
    return pl.pallas_call(
        kernel,
        name=name,
        compiler_params=pltpu.CompilerParams(vmem_limit_bytes=LIMIT),
        cost_estimate=pl.CostEstimate(flops=flops, bytes_accessed=size, transcendentals=0),
        in_specs=specs or [VMEM] * len(operands),
        out_specs=out_specs or [VMEM] * len(outs),
        out_shape=outs,
        **kwargs,
    )(*operands)


def in_hbm(value):
    return pltpu.with_memory_space_constraint(value, pltpu.HBM)


def stack(parts, cuts):
    rows = parts[0].shape[0]

    def kernel(*refs):
        ins, outs = refs[: len(parts)], refs[len(parts) :]
        for (at, span), out in zip(cuts, outs):
            for n, part in enumerate(ins):
                out[n * rows : (n + 1) * rows] = part[:, at : at + span]

    return call(
        kernel,
        "stack",
        0,
        sum(4 * rows * len(parts) * span for _, span in cuts),
        parts,
        [jax.ShapeDtypeStruct((rows * len(parts), span), jnp.bfloat16) for _, span in cuts],
    )


def gate_up(pieces, weights, at, span, sums, finish):
    group = pieces[0].shape[0]
    rows = RING * group
    units = weights[0].shape[0]
    block = math.gcd(span, 1024)
    steps = span // block
    opening, closing = sums is None, finish is not None

    def kernel(*refs):
        refs = list(refs)
        parts, loads, refs = refs[:RING], refs[RING : RING + 4], refs[RING + 4 :]
        before = None if opening else refs.pop(0)
        if closing:
            mixing, scalars, out, total, x = refs
        else:
            total, x = refs
        step = pl.program_id(0)

        @pl.when(step == 0)
        def _():
            total[...] = jnp.zeros(total.shape, total.dtype) if opening else before[...]

        for n, part in enumerate(parts):
            x[n * group : (n + 1) * group] = part[...]
        for n, weight in enumerate(loads):
            total[n] += lax.dot_general(
                x[...], weight[...], BY_ROWS, preferred_element_type=jnp.float32
            )

        if closing:

            @pl.when(step == steps - 1)
            def _():
                local = []
                for n in (0, 2):
                    gate, up = total[n], total[n + 1]
                    hidden = (gate / (1.0 + jnp.exp(-gate)) * up).astype(jnp.bfloat16)
                    local.append(dot(hidden, mixing[...]))
                own, other = local
                turn = scalars[0]
                out[:, :units] = (other + turn * own).astype(jnp.bfloat16)
                out[:, units:] = (own - turn * other).astype(jnp.bfloat16)

    operands = [*pieces, *[in_hbm(w) for w in weights]]
    specs = [pl.BlockSpec((group, block), lambda k: (0, k))] * RING
    specs += [pl.BlockSpec((units, block), lambda k: (0, k + at // block))] * 4
    scratch = [pltpu.VMEM((rows, block), jnp.bfloat16)]
    if not opening:
        operands.append(sums)
        specs.append(VMEM)
    if closing:
        operands += finish
        specs += [VMEM, SCALARS]
        out = jax.ShapeDtypeStruct((rows, 2 * units), jnp.bfloat16)
        scratch = [pltpu.VMEM((4, rows, units), jnp.float32)] + scratch
    else:
        out = jax.ShapeDtypeStruct((4, rows, units), jnp.float32)
    return call(
        kernel,
        "gate_up",
        8 * rows * units * span,
        8 * units * span,
        operands,
        [out],
        specs,
        grid=(steps,),
        scratch_shapes=scratch,
    )[0]


def combine(parts, scalars, first_scalar, major):
    rows, width = parts[0].shape
    slot = rows // (RING * RING)

    def kernel(*refs):
        came, factors, out = refs[:RING], refs[RING], refs[RING + 1]
        for i in range(RING):
            for j in range(RING):
                total = 0.0
                for s in range(RING):
                    where = ((i - s) % RING, j) if major else (i, (j - s) % RING)
                    at = (where[0] * RING + where[1]) * slot
                    total = total + factors[first_scalar + s] * came[s][at : at + slot].astype(
                        jnp.float32
                    )
                at = (i * RING + j) * slot
                out[at : at + slot] = total.astype(jnp.bfloat16)

    return call(
        kernel,
        "combine",
        0,
        10 * rows * width,
        [*parts, scalars],
        [jax.ShapeDtypeStruct((rows, width), jnp.bfloat16)],
        [VMEM] * RING + [SCALARS],
    )[0]


def down(value, weights, at, span):
    rows, units = value.shape[0], weights[0].shape[0]
    group = rows // RING
    block = math.gcd(span, 2048)

    def kernel(held, loaded, loaded_other, *outs):
        product = dot(held[:, :units], loaded[...]) + dot(held[:, units:], loaded_other[...])
        product = product.astype(jnp.bfloat16)
        for n, out in enumerate(outs):
            out[...] = product[n * group : (n + 1) * group]

    return call(
        kernel,
        "down",
        4 * rows * units * span,
        4 * units * span,
        [value, *[in_hbm(w) for w in weights]],
        [jax.ShapeDtypeStruct((group, span), jnp.bfloat16)] * RING,
        [pl.BlockSpec(value.shape, lambda k: (0, 0))]
        + [pl.BlockSpec((units, block), lambda k: (0, k + at // block))] * 2,
        grid=(span // block,),
        out_specs=[pl.BlockSpec((group, block), lambda k: (0, k))] * RING,
    )


def fold(sides):
    count = len(sides[0])
    group = sides[0][0].shape[0]
    rows = group // RING
    width = sum(parts[0].shape[1] for parts in sides)

    def kernel(*refs):
        ins, outs = refs[: count * len(sides)], refs[count * len(sides) :]
        start = 0
        for n in range(len(sides)):
            parts = ins[count * n : count * (n + 1)]
            stop = start + parts[0].shape[1]
            for m, out in enumerate(outs):
                at = slice(m * rows, (m + 1) * rows)
                total = sum(part[at].astype(jnp.float32) for part in parts)
                out[:, start:stop] = total.astype(jnp.bfloat16)
            start = stop

    return call(
        kernel,
        "fold",
        0,
        10 * group * width,
        [part for parts in sides for part in parts],
        [jax.ShapeDtypeStruct((rows, width), jnp.bfloat16)] * RING,
    )


def to_steps(parts, along):
    return parts[0], send(parts[1], along(1)), send(parts[2], along(2)), send(parts[3], along(-1))


def body(tokens, gate_weight, up_weight, down_weight, mixing):
    width = tokens.shape[1]
    index = lax.axis_index("tensor")
    scalars = lax.dynamic_index_in_dim(jnp.asarray(scalar_table()), index, keepdims=False)

    gate, up = gate_weight.T, up_weight.T
    weights = (gate, up, send(gate, SIBLING), send(up, SIBLING))

    cuts = cuts_of(GATHER_SPANS, width)
    blocks = stack((tokens, *from_steps(tokens, along_first)), cuts)
    value = None
    for n, (at, span) in enumerate(cuts):
        pieces = (blocks[n], *from_steps(blocks[n], along_second))
        finish = (mixing, scalars) if n == len(cuts) - 1 else None
        value = gate_up(pieces, weights, at, span, value, finish)

    down_other = send(after(down_weight, value), SIBLING)

    value = combine((value, *from_steps(value, along_first)), scalars, 1, False)
    value = combine((value, *from_steps(value, along_second)), scalars, 1 + RING, True)

    half = width // 2
    sides = [
        to_steps(down(value, (down_weight, down_other), at, half), along_second)
        for at in (0, half)
    ]
    parts = to_steps(fold(sides), along_first)
    return sum(part.astype(jnp.float32) for part in parts).astype(jnp.bfloat16)


def solution(mesh):
    in_specs = (
        P(("dp", "tensor"), None),
        P(None, "tensor"),
        P(None, "tensor"),
        P("tensor", None),
        P(),
    )
    out_specs = P(("dp", "tensor"), None)
    return jax.shard_map(body, mesh=mesh, in_specs=in_specs, out_specs=out_specs, check_vma=False)
```

```python
import math

import jax
import jax.numpy as jnp
import numpy as np
from jax import lax
from jax.experimental import pallas as pl
from jax.experimental.pallas import tpu as pltpu
from jax.sharding import PartitionSpec as P

RING = 4
PLACES = [(x, y, c) for x in range(RING) for y in range(RING) for c in range(2)]
GATHER_SPANS = (1, 1)
LIMIT = 40 * 2**20
SMALL = 16 * 2**20
BY_ROWS = (((1,), (1,)), ((), ()))


def place(x, y, c):
    return (x % RING) * RING * 2 + (y % RING) * 2 + c


def along_first(d):
    return [
        (place(x, y, c), place(x + d, y, c) if c == 0 else place(x, y + d, c))
        for x, y, c in PLACES
    ]


def along_second(d):
    return [
        (place(x, y, c), place(x + d, y, c) if c == 1 else place(x, y + d, c))
        for x, y, c in PLACES
    ]


SIBLING = [(place(x, y, c), place(x, y, 1 - c)) for x, y, c in PLACES]


def send(value, pairs):
    return lax.ppermute(value, "tensor", pairs)


def from_steps(value, along):
    return send(value, along(-1)), send(value, along(2)), send(value, along(1))


def after(value, *others):
    return lax.optimization_barrier((value, *others))[0]


def dot(a, b):
    return jnp.dot(a, b, preferred_element_type=jnp.float32)


def scalar_table():
    def sign(row, column):
        return 1.0 - 2.0 * (bin(row & column).count("1") % 2)

    rows = []
    for x, y, c in PLACES:
        first, second = (x, y) if c == 0 else (y, x)
        row = [1.0 - 2.0 * c]
        row += [sign(first, (first + s) % RING) for s in range(RING)]
        row += [
            sign(second, (second + s) % RING) / math.sqrt(2 * RING * RING) for s in range(RING)
        ]
        rows.append(row + [0.0] * (16 - len(row)))
    return np.array(rows, np.float32)


def cuts_of(shares, total):
    widths = [w * total // sum(shares) for w in shares]
    starts = [sum(widths[:n]) for n in range(len(widths))]
    return list(zip(starts, widths))


VMEM = pl.BlockSpec(memory_space=pltpu.VMEM)
SCALARS = pl.BlockSpec(memory_space=pltpu.SMEM)


def call(kernel, name, flops, size, operands, outs, specs=None, limit=SMALL, **kwargs):
    return pl.pallas_call(
        kernel,
        name=name,
        compiler_params=pltpu.CompilerParams(vmem_limit_bytes=limit),
        cost_estimate=pl.CostEstimate(flops=flops, bytes_accessed=size, transcendentals=0),
        in_specs=specs or [VMEM] * len(operands),
        out_specs=[VMEM] * len(outs),
        out_shape=outs,
        **kwargs,
    )(*operands)


def in_hbm(value):
    return pltpu.with_memory_space_constraint(value, pltpu.HBM)


def load(value, at, span):
    def kernel(value, out, sem):
        copy = pltpu.make_async_copy(value.at[:, pl.ds(at, span)], out, sem)
        copy.start()
        copy.wait()

    return pl.pallas_call(
        kernel,
        name="load",
        compiler_params=pltpu.CompilerParams(vmem_limit_bytes=SMALL),
        cost_estimate=pl.CostEstimate(
            flops=0, bytes_accessed=4 * value.shape[0] * span, transcendentals=0
        ),
        in_specs=[pl.BlockSpec(memory_space=pltpu.HBM)],
        out_specs=VMEM,
        out_shape=pltpu.VMEM((value.shape[0], span), value.dtype),
        scratch_shapes=[pltpu.SemaphoreType.DMA],
    )(in_hbm(value))


def stack(parts, cuts):
    rows = parts[0].shape[0]

    def kernel(*refs):
        ins, outs = refs[: len(parts)], refs[len(parts) :]
        for (at, span), out in zip(cuts, outs):
            for n, part in enumerate(ins):
                out[n * rows : (n + 1) * rows] = part[:, at : at + span]

    return call(
        kernel,
        "stack",
        0,
        sum(4 * rows * len(parts) * span for _, span in cuts),
        parts,
        [jax.ShapeDtypeStruct((rows * len(parts), span), jnp.bfloat16) for _, span in cuts],
    )


def gate_up(pieces, close, weights, at, span, sums, finish):
    group = pieces[0].shape[0]
    rows = RING * group
    units = weights[0].shape[0]
    block = math.gcd(span, 1024)
    steps = span // block
    opening, closing = sums is None, finish is not None

    def kernel(*refs):
        refs = list(refs)
        parts, loads, refs = refs[:RING], refs[RING : RING + 4], refs[RING + 4 :]
        before = None if opening else refs.pop(0)
        if closing:
            mixing, scalars, out, total, x = refs
        else:
            total, x = refs
        step = pl.program_id(0)

        @pl.when(step == 0)
        def _():
            total[...] = jnp.zeros(total.shape, total.dtype) if opening else before[...]

        for n, part in enumerate(parts):
            x[n * group : (n + 1) * group] = part[...]
        here = pl.ds(pl.multiple_of(step * block, block), block)
        for n, weight in enumerate(loads):
            total[n] += lax.dot_general(
                x[...],
                weight[:, here] if n < len(close) else weight[...],
                BY_ROWS,
                preferred_element_type=jnp.float32,
            )

        if closing:

            @pl.when(step == steps - 1)
            def _():
                local = []
                for n in (0, 2):
                    gate, up = total[n], total[n + 1]
                    hidden = (gate / (1.0 + jnp.exp(-gate)) * up).astype(jnp.bfloat16)
                    local.append(dot(hidden, mixing[...]))
                own, other = local
                turn = scalars[0]
                out[:, :units] = (other + turn * own).astype(jnp.bfloat16)
                out[:, units:] = (own - turn * other).astype(jnp.bfloat16)

    operands = [*pieces, *close, *[in_hbm(w) for w in weights[len(close) :]]]
    specs = [pl.BlockSpec((group, block), lambda k: (0, k))] * RING
    specs += [VMEM] * len(close)
    streamed = pl.BlockSpec((units, block), lambda k: (0, k + at // block))
    specs += [streamed] * (4 - len(close))
    scratch = [pltpu.VMEM((rows, block), jnp.bfloat16)]
    if not opening:
        operands.append(sums)
        specs.append(VMEM)
    if closing:
        operands += finish
        specs += [VMEM, SCALARS]
        out = jax.ShapeDtypeStruct((rows, 2 * units), jnp.bfloat16)
        scratch = [pltpu.VMEM((4, rows, units), jnp.float32)] + scratch
    else:
        out = jax.ShapeDtypeStruct((4, rows, units), jnp.float32)
    return call(
        kernel,
        "gate_up",
        8 * rows * units * span,
        8 * units * span,
        operands,
        [out],
        specs,
        LIMIT,
        grid=(steps,),
        scratch_shapes=scratch,
    )[0]


def combine(parts, scalars, first_scalar, major):
    rows, width = parts[0].shape
    slot = rows // (RING * RING)

    def kernel(*refs):
        came, factors, out = refs[:RING], refs[RING], refs[RING + 1]
        for i in range(RING):
            for j in range(RING):
                total = 0.0
                for s in range(RING):
                    where = ((i - s) % RING, j) if major else (i, (j - s) % RING)
                    at = (where[0] * RING + where[1]) * slot
                    total = total + factors[first_scalar + s] * came[s][at : at + slot].astype(
                        jnp.float32
                    )
                at = (i * RING + j) * slot
                out[at : at + slot] = total.astype(jnp.bfloat16)

    return call(
        kernel,
        "combine",
        0,
        10 * rows * width,
        [*parts, scalars],
        [jax.ShapeDtypeStruct((rows, width), jnp.bfloat16)],
        [VMEM] * RING + [SCALARS],
    )[0]


def down(value, weights, at, span):
    rows, units = value.shape[0], weights[0].shape[0]
    group = rows // RING
    block = min(span, 512)

    def kernel(held, loaded, loaded_other, *outs):
        for start in range(0, span, block):
            where = slice(at + start, at + start + block)
            product = dot(held[:, :units], loaded[:, where]) + dot(
                held[:, units:], loaded_other[:, where]
            )
            product = product.astype(jnp.bfloat16)
            for n, out in enumerate(outs):
                out[:, start : start + block] = product[n * group : (n + 1) * group]

    return call(
        kernel,
        "down",
        4 * rows * units * span,
        4 * units * span,
        [value, *weights],
        [jax.ShapeDtypeStruct((group, span), jnp.bfloat16)] * RING,
    )


def fold(sides):
    count = len(sides[0])
    group = sides[0][0].shape[0]
    rows = group // RING
    width = sum(parts[0].shape[1] for parts in sides)

    def kernel(*refs):
        ins, outs = refs[: count * len(sides)], refs[count * len(sides) :]
        start = 0
        for n in range(len(sides)):
            parts = ins[count * n : count * (n + 1)]
            stop = start + parts[0].shape[1]
            for m, out in enumerate(outs):
                at = slice(m * rows, (m + 1) * rows)
                total = sum(part[at].astype(jnp.float32) for part in parts)
                out[:, start:stop] = total.astype(jnp.bfloat16)
            start = stop

    return call(
        kernel,
        "fold",
        0,
        10 * group * width,
        [part for parts in sides for part in parts],
        [jax.ShapeDtypeStruct((rows, width), jnp.bfloat16)] * RING,
    )


def to_steps(parts, along):
    return parts[0], send(parts[1], along(1)), send(parts[2], along(2)), send(parts[3], along(-1))


def body(tokens, gate_weight, up_weight, down_weight, mixing):
    width = tokens.shape[1]
    index = lax.axis_index("tensor")
    scalars = lax.dynamic_index_in_dim(jnp.asarray(scalar_table()), index, keepdims=False)

    gate, up = gate_weight.T, up_weight.T
    cuts = cuts_of(GATHER_SPANS, width)
    held = [load(gate, *cuts[-1]), load(up, *cuts[-1])]
    weights = [gate, up, send(gate, SIBLING), send(up, SIBLING)]

    near = from_steps(tokens, along_first)
    blocks = stack((after(tokens, *held), *near), cuts)
    value = None
    for n, (at, span) in enumerate(cuts):
        pieces = (blocks[n], *from_steps(blocks[n], along_second))
        finish = (mixing, scalars) if n == len(cuts) - 1 else None
        value = gate_up(pieces, held if finish else [], weights, at, span, value, finish)

    down_other = send(after(down_weight, value), SIBLING)

    value = combine((value, *from_steps(value, along_first)), scalars, 1, False)
    down_own = load(down_weight, 0, width)
    value = after(value, down_own)
    value = combine((value, *from_steps(value, along_second)), scalars, 1 + RING, True)

    half = width // 2
    sides = [
        to_steps(down(value, (down_own, down_other), at, half), along_second)
        for at in (0, half)
    ]
    parts = to_steps(fold(sides), along_first)
    return sum(part.astype(jnp.float32) for part in parts).astype(jnp.bfloat16)


def solution(mesh):
    in_specs = (
        P(("dp", "tensor"), None),
        P(None, "tensor"),
        P(None, "tensor"),
        P("tensor", None),
        P(),
    )
    out_specs = P(("dp", "tensor"), None)
    return jax.shard_map(body, mesh=mesh, in_specs=in_specs, out_specs=out_specs, check_vma=False)
```

```python
import math

import jax
import jax.numpy as jnp
import numpy as np
from jax import lax
from jax.experimental import pallas as pl
from jax.experimental.pallas import tpu as pltpu
from jax.sharding import PartitionSpec as P

RING = 4
ORDER = (0, 2, 1, 3)
PLACES = [(x, y, c) for x in range(RING) for y in range(RING) for c in range(2)]
GATHER_SPANS = (1, 1)
OUT_SPANS = (1, 1)
LIMIT = 24 * 2**20
SMALL = 16 * 2**20
BY_ROWS = (((1,), (1,)), ((), ()))


def place(x, y, c):
    return (x % RING) * RING * 2 + (y % RING) * 2 + c


def along_first(d):
    return [
        (place(x, y, c), place(x + d, y, c) if c == 0 else place(x, y + d, c))
        for x, y, c in PLACES
    ]


def along_second(d):
    return [
        (place(x, y, c), place(x + d, y, c) if c == 1 else place(x, y + d, c))
        for x, y, c in PLACES
    ]


SIBLING = [(place(x, y, c), place(x, y, 1 - c)) for x, y, c in PLACES]


def send(value, pairs):
    return lax.ppermute(value, "tensor", pairs)


def from_steps(value, along):
    return send(value, along(2)), send(value, along(-1)), send(value, along(1))


def after(value, *others):
    return lax.optimization_barrier((value, *others))[0]


def dot(a, b):
    return jnp.dot(a, b, preferred_element_type=jnp.float32)


def scalar_table():
    def sign(row, column):
        return 1.0 - 2.0 * (bin(row & column).count("1") % 2)

    rows = []
    for x, y, c in PLACES:
        first, second = (x, y) if c == 0 else (y, x)
        row = [1.0 - 2.0 * c]
        row += [sign(first, (first + s) % RING) for s in range(RING)]
        row += [
            sign(second, (second + s) % RING) / math.sqrt(2 * RING * RING) for s in range(RING)
        ]
        rows.append(row + [0.0] * (16 - len(row)))
    return np.array(rows, np.float32)


def cuts_of(shares, total):
    widths = [w * total // sum(shares) for w in shares]
    starts = [sum(widths[:n]) for n in range(len(widths))]
    return list(zip(starts, widths))


VMEM = pl.BlockSpec(memory_space=pltpu.VMEM)
SCALARS = pl.BlockSpec(memory_space=pltpu.SMEM)


def call(kernel, name, flops, size, operands, outs, specs=None, limit=SMALL, **kwargs):
    return pl.pallas_call(
        kernel,
        name=name,
        compiler_params=pltpu.CompilerParams(vmem_limit_bytes=limit),
        cost_estimate=pl.CostEstimate(flops=flops, bytes_accessed=size, transcendentals=0),
        in_specs=specs or [VMEM] * len(operands),
        out_specs=[VMEM] * len(outs),
        out_shape=outs,
        **kwargs,
    )(*operands)


def in_hbm(value):
    return pltpu.with_memory_space_constraint(value, pltpu.HBM)


def load(values, at, span):
    count = len(values)

    def kernel(*refs):
        sems = refs[-1]
        copies = [
            pltpu.make_async_copy(refs[n].at[:, pl.ds(at, span)], refs[count + n], sems.at[n])
            for n in range(count)
        ]
        for copy in copies:
            copy.start()
        for copy in copies:
            copy.wait()

    return pl.pallas_call(
        kernel,
        name="load",
        compiler_params=pltpu.CompilerParams(vmem_limit_bytes=SMALL),
        cost_estimate=pl.CostEstimate(
            flops=0,
            bytes_accessed=sum(4 * value.shape[0] * span for value in values),
            transcendentals=0,
        ),
        in_specs=[pl.BlockSpec(memory_space=pltpu.HBM)] * count,
        out_specs=[VMEM] * count,
        out_shape=[pltpu.VMEM((value.shape[0], span), value.dtype) for value in values],
        scratch_shapes=[pltpu.SemaphoreType.DMA((count,))],
    )(*[in_hbm(value) for value in values])


def stack(parts, cuts):
    rows = parts[0].shape[0]

    def kernel(*refs):
        ins, outs = refs[: len(parts)], refs[len(parts) :]
        for (at, span), out in zip(cuts, outs):
            for n, part in zip(ORDER, ins):
                out[n * rows : (n + 1) * rows] = part[:, at : at + span]

    return call(
        kernel,
        "stack",
        0,
        sum(4 * rows * len(parts) * span for _, span in cuts),
        parts,
        [jax.ShapeDtypeStruct((rows * len(parts), span), jnp.bfloat16) for _, span in cuts],
    )


def gate_up(pieces, close, weights, at, span, sums, finish):
    group = pieces[0].shape[0]
    rows = RING * group
    units = weights[0].shape[0]
    block = math.gcd(span, 2048)
    steps = span // block
    opening, closing = sums is None, finish is not None
    count = len(close)

    def kernel(*refs):
        refs = list(refs)
        parts, near = refs[:RING], refs[RING : RING + count]
        far = refs[RING + count : RING + 4]
        refs = refs[RING + 4 :]
        x, held, sems, refs = refs[-3], refs[-2], refs[-1], refs[:-3]
        before = None if opening else refs.pop(0)
        if closing:
            mixing, scalars, out, total = refs
        else:
            (total,) = refs
        copies = [
            [
                pltpu.make_async_copy(
                    load.at[:, pl.ds(at + step * block, block)], held.at[step, n], sems.at[step, n]
                )
                for step in range(steps)
            ]
            for n, load in enumerate(far)
        ]
        for step in range(steps):
            for n in range(4 - count):
                copies[n][step].start()
        for n, part in zip(ORDER, parts):
            x[n * group : (n + 1) * group] = part[...]
        for n in range(count):
            product = lax.dot_general(
                x[...], near[n][...], BY_ROWS, preferred_element_type=jnp.float32
            )
            total[n] = product if opening else before[n] + product
        for step in range(steps):
            here = x[:, step * block : (step + 1) * block]
            for n in range(4 - count):
                copies[n][step].wait()
                product = lax.dot_general(
                    here, held[step, n], BY_ROWS, preferred_element_type=jnp.float32
                )
                if step > 0:
                    total[count + n] += product
                else:
                    total[count + n] = product if opening else before[count + n] + product
        if closing:
            local = []
            for n in (0, 2):
                gate, up = total[n], total[n + 1]
                hidden = (gate / (1.0 + jnp.exp(-gate)) * up).astype(jnp.bfloat16)
                local.append(dot(hidden, mixing[...]))
            own, other = local
            turn = scalars[0]
            out[:, :units] = (other + turn * own).astype(jnp.bfloat16)
            out[:, units:] = (own - turn * other).astype(jnp.bfloat16)

    operands = [*pieces, *close, *[in_hbm(w) for w in weights]]
    specs = [VMEM] * (RING + count) + [pl.BlockSpec(memory_space=pltpu.HBM)] * (4 - count)
    scratch = [
        pltpu.VMEM((rows, span), jnp.bfloat16),
        pltpu.VMEM((steps, 4 - count, units, block), jnp.bfloat16),
        pltpu.SemaphoreType.DMA((steps, 4 - count)),
    ]
    if not opening:
        operands.append(sums)
        specs.append(VMEM)
    if closing:
        operands += finish
        specs += [VMEM, SCALARS]
        out = jax.ShapeDtypeStruct((rows, 2 * units), jnp.bfloat16)
        scratch = [pltpu.VMEM((4, rows, units), jnp.float32)] + scratch
    else:
        out = jax.ShapeDtypeStruct((4, rows, units), jnp.float32)
    return call(
        kernel,
        "gate_up",
        8 * rows * units * span,
        8 * units * span,
        operands,
        [out],
        specs,
        LIMIT,
        scratch_shapes=scratch,
    )[0]


def combine(parts, scalars, first_scalar, major):
    rows, width = parts[0].shape
    slot = rows // (RING * RING)

    def kernel(*refs):
        came = dict(zip(ORDER, refs[:RING]))
        factors, out = refs[RING], refs[RING + 1]
        for i in range(RING):
            for j in range(RING):
                total = 0.0
                for s in range(RING):
                    where = ((i - s) % RING, j) if major else (i, (j - s) % RING)
                    at = (where[0] * RING + where[1]) * slot
                    total = total + factors[first_scalar + s] * came[s][at : at + slot].astype(
                        jnp.float32
                    )
                at = (i * RING + j) * slot
                out[at : at + slot] = total.astype(jnp.bfloat16)

    return call(
        kernel,
        "combine",
        0,
        10 * rows * width,
        [*parts, scalars],
        [jax.ShapeDtypeStruct((rows, width), jnp.bfloat16)],
        [VMEM] * RING + [SCALARS],
    )[0]


def down(value, weights, at, span):
    rows, units = value.shape[0], weights[0].shape[0]
    group = rows // RING
    block = min(span, 512)

    def kernel(held, loaded, loaded_other, *outs):
        for start in range(0, span, block):
            where = slice(at + start, at + start + block)
            product = dot(held[:, :units], loaded[:, where]) + dot(
                held[:, units:], loaded_other[:, where]
            )
            product = product.astype(jnp.bfloat16)
            for n, out in enumerate(outs):
                out[:, start : start + block] = product[n * group : (n + 1) * group]

    return call(
        kernel,
        "down",
        4 * rows * units * span,
        4 * units * span,
        [value, *weights],
        [jax.ShapeDtypeStruct((group, span), jnp.bfloat16)] * RING,
    )


def fold(sides):
    count = len(sides[0])
    group = sides[0][0].shape[0]
    rows = group // RING
    width = sum(parts[0].shape[1] for parts in sides)

    def kernel(*refs):
        ins, outs = refs[: count * len(sides)], refs[count * len(sides) :]
        start = 0
        for n in range(len(sides)):
            parts = ins[count * n : count * (n + 1)]
            stop = start + parts[0].shape[1]
            for m, out in enumerate(outs):
                at = slice(m * rows, (m + 1) * rows)
                total = sum(part[at].astype(jnp.float32) for part in parts)
                out[:, start:stop] = total.astype(jnp.bfloat16)
            start = stop

    return call(
        kernel,
        "fold",
        0,
        10 * group * width,
        [part for parts in sides for part in parts],
        [jax.ShapeDtypeStruct((rows, width), jnp.bfloat16)] * RING,
    )


def to_steps(parts, along):
    return parts[0], send(parts[2], along(2)), send(parts[1], along(1)), send(parts[3], along(-1))


def body(tokens, gate_weight, up_weight, down_weight, mixing):
    width = tokens.shape[1]
    index = lax.axis_index("tensor")
    scalars = lax.dynamic_index_in_dim(jnp.asarray(scalar_table()), index, keepdims=False)

    gate, up = gate_weight.T, up_weight.T
    cuts = cuts_of(GATHER_SPANS, width)
    others = send(gate, SIBLING), send(up, SIBLING)

    near = from_steps(tokens, along_first)
    (own,) = load((tokens,), 0, width)
    blocks = stack((own, *near), cuts)
    value = None
    for n, (at, span) in enumerate(cuts):
        pieces = (blocks[n], *from_steps(blocks[n], along_second))
        finish = (mixing, scalars) if n == len(cuts) - 1 else None
        if n == 0:
            value = gate_up(pieces, (), (gate, up, *others), at, span, value, finish)
        else:
            close = load((after(gate, value), up), at, span)
            value = gate_up(pieces, close, others, at, span, value, finish)

    down_other = send(after(down_weight, value), SIBLING)
    (down_own,) = load((down_weight,), 0, width)
    value = combine((value, *from_steps(value, along_first)), scalars, 1, False)
    value = after(value, down_own)
    value = combine((value, *from_steps(value, along_second)), scalars, 1 + RING, True)

    sides = [
        to_steps(down(value, (down_own, down_other), at, span), along_second)
        for at, span in cuts_of(OUT_SPANS, width)
    ]
    parts = to_steps(fold(sides), along_first)
    return sum(part.astype(jnp.float32) for part in parts).astype(jnp.bfloat16)


def solution(mesh):
    in_specs = (
        P(("dp", "tensor"), None),
        P(None, "tensor"),
        P(None, "tensor"),
        P("tensor", None),
        P(),
    )
    out_specs = P(("dp", "tensor"), None)
    return jax.shard_map(body, mesh=mesh, in_specs=in_specs, out_specs=out_specs, check_vma=False)
```

```python
import math

import jax
import jax.numpy as jnp
import numpy as np
from jax import lax
from jax.experimental import pallas as pl
from jax.experimental.pallas import tpu as pltpu
from jax.sharding import PartitionSpec as P

RING = 4
TOKEN_ORDER = (0, 2, 1, 3)
ORDER = (0, 1, 3, 2)
PLACES = [(x, y, c) for x in range(RING) for y in range(RING) for c in range(2)]
GATHER_SPANS = (1, 1)
OUT_SPANS = (1, 1)
LIMIT = 24 * 2**20
SMALL = 16 * 2**20
BY_ROWS = (((1,), (1,)), ((), ()))


def place(x, y, c):
    return (x % RING) * RING * 2 + (y % RING) * 2 + c


def along_first(d):
    return [
        (place(x, y, c), place(x + d, y, c) if c == 0 else place(x, y + d, c))
        for x, y, c in PLACES
    ]


def along_second(d):
    return [
        (place(x, y, c), place(x + d, y, c) if c == 1 else place(x, y + d, c))
        for x, y, c in PLACES
    ]


SIBLING = [(place(x, y, c), place(x, y, 1 - c)) for x, y, c in PLACES]


def send(value, pairs):
    return lax.ppermute(value, "tensor", pairs)


def from_steps(value, along, order):
    return [send(value, along({1: -1, 2: 2, 3: 1}[step])) for step in order[1:]]


def after(value, *others):
    return lax.optimization_barrier((value, *others))[0]


def dot(a, b):
    return jnp.dot(a, b, preferred_element_type=jnp.float32)


def scalar_table():
    def sign(row, column):
        return 1.0 - 2.0 * (bin(row & column).count("1") % 2)

    rows = []
    for x, y, c in PLACES:
        first, second = (x, y) if c == 0 else (y, x)
        row = [1.0 - 2.0 * c]
        row += [sign(first, (first + s) % RING) for s in range(RING)]
        row += [
            sign(second, (second + s) % RING) / math.sqrt(2 * RING * RING) for s in range(RING)
        ]
        rows.append(row + [0.0] * (16 - len(row)))
    return np.array(rows, np.float32)


def cuts_of(shares, total):
    widths = [w * total // sum(shares) for w in shares]
    starts = [sum(widths[:n]) for n in range(len(widths))]
    return list(zip(starts, widths))


VMEM = pl.BlockSpec(memory_space=pltpu.VMEM)
SCALARS = pl.BlockSpec(memory_space=pltpu.SMEM)


def call(kernel, name, flops, size, operands, outs, specs=None, limit=SMALL, **kwargs):
    return pl.pallas_call(
        kernel,
        name=name,
        compiler_params=pltpu.CompilerParams(vmem_limit_bytes=limit),
        cost_estimate=pl.CostEstimate(flops=flops, bytes_accessed=size, transcendentals=0),
        in_specs=specs or [VMEM] * len(operands),
        out_specs=[VMEM] * len(outs),
        out_shape=outs,
        **kwargs,
    )(*operands)


def in_hbm(value):
    return pltpu.with_memory_space_constraint(value, pltpu.HBM)


def load(values, at, span):
    count = len(values)

    def kernel(*refs):
        sems = refs[-1]
        copies = [
            pltpu.make_async_copy(refs[n].at[:, pl.ds(at, span)], refs[count + n], sems.at[n])
            for n in range(count)
        ]
        for copy in copies:
            copy.start()
        for copy in copies:
            copy.wait()

    return pl.pallas_call(
        kernel,
        name="load",
        compiler_params=pltpu.CompilerParams(vmem_limit_bytes=SMALL),
        cost_estimate=pl.CostEstimate(
            flops=0,
            bytes_accessed=sum(4 * value.shape[0] * span for value in values),
            transcendentals=0,
        ),
        in_specs=[pl.BlockSpec(memory_space=pltpu.HBM)] * count,
        out_specs=[VMEM] * count,
        out_shape=[pltpu.VMEM((value.shape[0], span), value.dtype) for value in values],
        scratch_shapes=[pltpu.SemaphoreType.DMA((count,))],
    )(*[in_hbm(value) for value in values])


def stack(parts, cuts):
    rows = parts[0].shape[0]

    def kernel(*refs):
        ins, outs = refs[: len(parts)], refs[len(parts) :]
        for (at, span), out in zip(cuts, outs):
            for n, part in zip(TOKEN_ORDER, ins):
                out[n * rows : (n + 1) * rows] = part[:, at : at + span]

    return call(
        kernel,
        "stack",
        0,
        sum(4 * rows * len(parts) * span for _, span in cuts),
        parts,
        [jax.ShapeDtypeStruct((rows * len(parts), span), jnp.bfloat16) for _, span in cuts],
    )


def local(gate, up, mixing):
    hidden = (gate / (1.0 + jnp.exp(-gate)) * up).astype(jnp.bfloat16)
    return dot(hidden, mixing[...])


def gate_up(pieces, close, weights, at, span, sums, finish):
    group = pieces[0].shape[0]
    rows = RING * group
    units = weights[0].shape[0]
    block = math.gcd(span, 2048)
    steps = span // block
    opening, closing = sums is None, finish is not None
    count = len(close)

    def kernel(*refs):
        refs = list(refs)
        parts, near = refs[:RING], refs[RING : RING + count]
        far = refs[RING + count : RING + 4]
        refs = refs[RING + 4 :]
        x, held, sems, refs = refs[-3], refs[-2], refs[-1], refs[:-3]
        before = None if opening else refs.pop(0)
        if closing:
            mixing, scalars, out, total = refs
        else:
            (total,) = refs
        copies = [
            [
                pltpu.make_async_copy(
                    load.at[:, pl.ds(at + step * block, block)], held.at[step, n], sems.at[step, n]
                )
                for step in range(steps)
            ]
            for n, load in enumerate(far)
        ]
        for step in range(steps):
            for n in range(4 - count):
                copies[n][step].start()
        for n, part in zip(ORDER, parts):
            x[n * group : (n + 1) * group] = part[...]
        for n in range(count):
            product = lax.dot_general(
                x[...], near[n][...], BY_ROWS, preferred_element_type=jnp.float32
            )
            total[n] = product if opening else before[n] + product
        if closing and count == 2:
            own = local(total[0], total[1], mixing)
        for step in range(steps):
            here = x[:, step * block : (step + 1) * block]
            for n in range(4 - count):
                copies[n][step].wait()
                product = lax.dot_general(
                    here, held[step, n], BY_ROWS, preferred_element_type=jnp.float32
                )
                if step > 0:
                    total[count + n] += product
                else:
                    total[count + n] = product if opening else before[count + n] + product
        if closing:
            if count != 2:
                own = local(total[0], total[1], mixing)
            other = local(total[2], total[3], mixing)
            turn = scalars[0]
            out[:, :units] = (other + turn * own).astype(jnp.bfloat16)
            out[:, units:] = (own - turn * other).astype(jnp.bfloat16)

    operands = [*pieces, *close, *[in_hbm(w) for w in weights]]
    specs = [VMEM] * (RING + count) + [pl.BlockSpec(memory_space=pltpu.HBM)] * (4 - count)
    scratch = [
        pltpu.VMEM((rows, span), jnp.bfloat16),
        pltpu.VMEM((steps, 4 - count, units, block), jnp.bfloat16),
        pltpu.SemaphoreType.DMA((steps, 4 - count)),
    ]
    if not opening:
        operands.append(sums)
        specs.append(VMEM)
    if closing:
        operands += finish
        specs += [VMEM, SCALARS]
        out = jax.ShapeDtypeStruct((rows, 2 * units), jnp.bfloat16)
        scratch = [pltpu.VMEM((4, rows, units), jnp.float32)] + scratch
    else:
        out = jax.ShapeDtypeStruct((4, rows, units), jnp.float32)
    return call(
        kernel,
        "gate_up",
        8 * rows * units * span,
        8 * units * span,
        operands,
        [out],
        specs,
        LIMIT if opening else SMALL,
        scratch_shapes=scratch,
    )[0]


def turn_rows(came, factors, first_scalar, major, out):
    slot = out.shape[0] // (RING * RING)
    for i in range(RING):
        for j in range(RING):
            total = 0.0
            for s in range(RING):
                where = ((i - s) % RING, j) if major else (i, (j - s) % RING)
                at = (where[0] * RING + where[1]) * slot
                total = total + factors[first_scalar + s] * came[s][at : at + slot].astype(
                    jnp.float32
                )
            at = (i * RING + j) * slot
            out[at : at + slot] = total.astype(jnp.bfloat16)


def down_rows(held, loaded, loaded_other, at, span, outs):
    units = loaded.shape[0]
    group = held.shape[0] // RING
    block = min(span, 512)
    for start in range(0, span, block):
        where = slice(at + start, at + start + block)
        product = dot(held[:, :units], loaded[:, where]) + dot(
            held[:, units:], loaded_other[:, where]
        )
        product = product.astype(jnp.bfloat16)
        for n, out in enumerate(outs):
            out[:, start : start + block] = product[n * group : (n + 1) * group]


def combine(parts, scalars, first_scalar, major):
    rows, width = parts[0].shape

    def kernel(*refs):
        came = dict(zip(ORDER, refs[:RING]))
        turn_rows(came, refs[RING], first_scalar, major, refs[RING + 1])

    return call(
        kernel,
        "combine",
        0,
        10 * rows * width,
        [*parts, scalars],
        [jax.ShapeDtypeStruct((rows, width), jnp.bfloat16)],
        [VMEM] * RING + [SCALARS],
    )[0]


def combine_down(parts, scalars, first_scalar, major, weights, at, span):
    rows, width = parts[0].shape

    def kernel(*refs):
        came = dict(zip(ORDER, refs[:RING]))
        factors, loaded, loaded_other, value, *outs = refs[RING:]
        turn_rows(came, factors, first_scalar, major, value)
        down_rows(value, loaded, loaded_other, at, span, outs)

    value, *outs = call(
        kernel,
        "combine_down",
        2 * rows * width * span,
        2 * width * span,
        [*parts, scalars, *weights],
        [jax.ShapeDtypeStruct((rows, width), jnp.bfloat16)]
        + [jax.ShapeDtypeStruct((rows // RING, span), jnp.bfloat16)] * RING,
        [VMEM] * RING + [SCALARS] + [VMEM] * 2,
    )
    return value, outs


def down(value, weights, at, span):
    rows, width = value.shape

    def kernel(held, loaded, loaded_other, *outs):
        down_rows(held, loaded, loaded_other, at, span, outs)

    return call(
        kernel,
        "down",
        2 * rows * width * span,
        2 * width * span,
        [value, *weights],
        [jax.ShapeDtypeStruct((rows // RING, span), jnp.bfloat16)] * RING,
    )


def fold(sides):
    count = len(sides[0])
    group = sides[0][0].shape[0]
    rows = group // RING
    width = sum(parts[0].shape[1] for parts in sides)

    def kernel(*refs):
        ins, outs = refs[: count * len(sides)], refs[count * len(sides) :]
        start = 0
        for n in range(len(sides)):
            parts = ins[count * n : count * (n + 1)]
            stop = start + parts[0].shape[1]
            for m, out in enumerate(outs):
                at = slice(m * rows, (m + 1) * rows)
                total = sum(part[at].astype(jnp.float32) for part in parts)
                out[:, start:stop] = total.astype(jnp.bfloat16)
            start = stop

    return call(
        kernel,
        "fold",
        0,
        10 * group * width,
        [part for parts in sides for part in parts],
        [jax.ShapeDtypeStruct((rows, width), jnp.bfloat16)] * RING,
    )


def to_steps(parts, along):
    return parts[0], send(parts[2], along(2)), send(parts[1], along(1)), send(parts[3], along(-1))


def body(tokens, gate_weight, up_weight, down_weight, mixing):
    width = tokens.shape[1]
    index = lax.axis_index("tensor")
    scalars = lax.dynamic_index_in_dim(jnp.asarray(scalar_table()), index, keepdims=False)

    gate, up = gate_weight.T, up_weight.T
    cuts = cuts_of(GATHER_SPANS, width)
    others = send(gate, SIBLING), send(up, SIBLING)

    near = from_steps(tokens, along_first, TOKEN_ORDER)
    (own,) = load((tokens,), 0, width)
    own = after(own, scalars)
    blocks = stack((own, *near), cuts)
    value = None
    for n, (at, span) in enumerate(cuts):
        pieces = (blocks[n], *from_steps(blocks[n], along_second, ORDER))
        finish = (mixing, scalars) if n == len(cuts) - 1 else None
        if n == 0:
            value = gate_up(pieces, (), (gate, up, *others), at, span, value, finish)
        else:
            close = load((after(gate, value), up), at, span)
            value = gate_up(pieces, close, others, at, span, value, finish)

    down_own = after(down_weight, value)
    down_other = send(down_own, SIBLING)
    value = combine((value, *from_steps(value, along_first, ORDER)), scalars, 1, False)
    left, right = cuts_of(OUT_SPANS, width)
    weights = (down_own, down_other)
    parts = (value, *from_steps(value, along_second, ORDER))
    value, partial = combine_down(parts, scalars, 1 + RING, True, weights, *left)
    sides = [to_steps(partial, along_second)]
    sides.append(to_steps(down(value, weights, *right), along_second))
    parts = to_steps(fold(sides), along_first)
    return sum(part.astype(jnp.float32) for part in parts).astype(jnp.bfloat16)


def solution(mesh):
    in_specs = (
        P(("dp", "tensor"), None),
        P(None, "tensor"),
        P(None, "tensor"),
        P("tensor", None),
        P(),
    )
    out_specs = P(("dp", "tensor"), None)
    return jax.shard_map(body, mesh=mesh, in_specs=in_specs, out_specs=out_specs, check_vma=False)
```

```python
import math

import jax
import jax.numpy as jnp
import numpy as np
from jax import lax
from jax.experimental import pallas as pl
from jax.experimental.pallas import tpu as pltpu
from jax.sharding import PartitionSpec as P

RING = 4
TOKEN_ORDER = (0, 2, 1, 3)
ORDER = (0, 1, 3, 2)
PLACES = [(x, y, c) for x in range(RING) for y in range(RING) for c in range(2)]
GATHER_SPANS = (1, 1)
OUT_SPANS = (3, 5)
LIMIT = 24 * 2**20
SMALL = 16 * 2**20
BY_ROWS = (((1,), (1,)), ((), ()))


def place(x, y, c):
    return (x % RING) * RING * 2 + (y % RING) * 2 + c


def along_first(d):
    return [
        (place(x, y, c), place(x + d, y, c) if c == 0 else place(x, y + d, c))
        for x, y, c in PLACES
    ]


def along_second(d):
    return [
        (place(x, y, c), place(x + d, y, c) if c == 1 else place(x, y + d, c))
        for x, y, c in PLACES
    ]


SIBLING = [(place(x, y, c), place(x, y, 1 - c)) for x, y, c in PLACES]


def send(value, pairs):
    return lax.ppermute(value, "tensor", pairs)


def from_steps(value, along, order):
    return [send(value, along({1: -1, 2: 2, 3: 1}[step])) for step in order[1:]]


def after(value, *others):
    return lax.optimization_barrier((value, *others))[0]


def dot(a, b):
    return jnp.dot(a, b, preferred_element_type=jnp.float32)


def scalar_table():
    def sign(row, column):
        return 1.0 - 2.0 * (bin(row & column).count("1") % 2)

    rows = []
    for x, y, c in PLACES:
        first, second = (x, y) if c == 0 else (y, x)
        row = [1.0 - 2.0 * c]
        row += [sign(first, (first + s) % RING) for s in range(RING)]
        row += [
            sign(second, (second + s) % RING) / math.sqrt(2 * RING * RING) for s in range(RING)
        ]
        rows.append(row + [0.0] * (16 - len(row)))
    return np.array(rows, np.float32)


def cuts_of(shares, total):
    widths = [w * total // sum(shares) for w in shares]
    starts = [sum(widths[:n]) for n in range(len(widths))]
    return list(zip(starts, widths))


VMEM = pl.BlockSpec(memory_space=pltpu.VMEM)
SCALARS = pl.BlockSpec(memory_space=pltpu.SMEM)


def call(kernel, name, flops, size, operands, outs, specs=None, limit=SMALL, **kwargs):
    return pl.pallas_call(
        kernel,
        name=name,
        compiler_params=pltpu.CompilerParams(vmem_limit_bytes=limit),
        cost_estimate=pl.CostEstimate(flops=flops, bytes_accessed=size, transcendentals=0),
        in_specs=specs or [VMEM] * len(operands),
        out_specs=[VMEM] * len(outs),
        out_shape=outs,
        **kwargs,
    )(*operands)


def in_hbm(value):
    return pltpu.with_memory_space_constraint(value, pltpu.HBM)


def load(values, at, span):
    count = len(values)

    def kernel(*refs):
        sems = refs[-1]
        copies = [
            pltpu.make_async_copy(refs[n].at[:, pl.ds(at, span)], refs[count + n], sems.at[n])
            for n in range(count)
        ]
        for copy in copies:
            copy.start()
        for copy in copies:
            copy.wait()

    return pl.pallas_call(
        kernel,
        name="load",
        compiler_params=pltpu.CompilerParams(vmem_limit_bytes=SMALL),
        cost_estimate=pl.CostEstimate(
            flops=0,
            bytes_accessed=sum(4 * value.shape[0] * span for value in values),
            transcendentals=0,
        ),
        in_specs=[pl.BlockSpec(memory_space=pltpu.HBM)] * count,
        out_specs=[VMEM] * count,
        out_shape=[pltpu.VMEM((value.shape[0], span), value.dtype) for value in values],
        scratch_shapes=[pltpu.SemaphoreType.DMA((count,))],
    )(*[in_hbm(value) for value in values])


def stack(parts, cuts):
    rows = parts[0].shape[0]

    def kernel(*refs):
        ins, outs = refs[: len(parts)], refs[len(parts) :]
        for (at, span), out in zip(cuts, outs):
            for n, part in zip(TOKEN_ORDER, ins):
                out[n * rows : (n + 1) * rows] = part[:, at : at + span]

    return call(
        kernel,
        "stack",
        0,
        sum(4 * rows * len(parts) * span for _, span in cuts),
        parts,
        [jax.ShapeDtypeStruct((rows * len(parts), span), jnp.bfloat16) for _, span in cuts],
    )


def local(gate, up, mixing):
    hidden = (gate / (1.0 + jnp.exp(-gate)) * up).astype(jnp.bfloat16)
    return dot(hidden, mixing[...])


def gate_up(pieces, close, weights, at, span, sums, finish):
    group = pieces[0].shape[0]
    rows = RING * group
    units = weights[0].shape[0]
    block = math.gcd(span, 2048)
    steps = span // block
    opening, closing = sums is None, finish is not None
    count = len(close)

    def kernel(*refs):
        refs = list(refs)
        parts, near = refs[:RING], refs[RING : RING + count]
        far = refs[RING + count : RING + 4]
        refs = refs[RING + 4 :]
        x, held, sems, refs = refs[-3], refs[-2], refs[-1], refs[:-3]
        before = None if opening else refs.pop(0)
        if closing:
            mixing, scalars, out, total = refs
        else:
            (total,) = refs
        copies = [
            [
                pltpu.make_async_copy(
                    load.at[:, pl.ds(at + step * block, block)], held.at[step, n], sems.at[step, n]
                )
                for step in range(steps)
            ]
            for n, load in enumerate(far)
        ]
        for step in range(steps):
            for n in range(4 - count):
                copies[n][step].start()
        for n, part in zip(ORDER, parts):
            x[n * group : (n + 1) * group] = part[...]
        for n in range(count):
            product = lax.dot_general(
                x[...], near[n][...], BY_ROWS, preferred_element_type=jnp.float32
            )
            total[n] = product if opening else before[n] + product
        if closing and count == 2:
            own = local(total[0], total[1], mixing)
        for step in range(steps):
            here = x[:, step * block : (step + 1) * block]
            for n in range(4 - count):
                copies[n][step].wait()
                product = lax.dot_general(
                    here, held[step, n], BY_ROWS, preferred_element_type=jnp.float32
                )
                if step > 0:
                    total[count + n] += product
                else:
                    total[count + n] = product if opening else before[count + n] + product
        if closing:
            if count != 2:
                own = local(total[0], total[1], mixing)
            other = local(total[2], total[3], mixing)
            turn = scalars[0]
            out[:, :units] = (other + turn * own).astype(jnp.bfloat16)
            out[:, units:] = (own - turn * other).astype(jnp.bfloat16)

    operands = [*pieces, *close, *[in_hbm(w) for w in weights]]
    specs = [VMEM] * (RING + count) + [pl.BlockSpec(memory_space=pltpu.HBM)] * (4 - count)
    scratch = [
        pltpu.VMEM((rows, span), jnp.bfloat16),
        pltpu.VMEM((steps, 4 - count, units, block), jnp.bfloat16),
        pltpu.SemaphoreType.DMA((steps, 4 - count)),
    ]
    if not opening:
        operands.append(sums)
        specs.append(VMEM)
    if closing:
        operands += finish
        specs += [VMEM, SCALARS]
        out = jax.ShapeDtypeStruct((rows, 2 * units), jnp.bfloat16)
        scratch = [pltpu.VMEM((4, rows, units), jnp.float32)] + scratch
    else:
        out = jax.ShapeDtypeStruct((4, rows, units), jnp.float32)
    return call(
        kernel,
        "gate_up",
        8 * rows * units * span,
        8 * units * span,
        operands,
        [out],
        specs,
        LIMIT if opening else SMALL,
        scratch_shapes=scratch,
    )[0]


def turn_rows(came, factors, first_scalar, major, out):
    slot = out.shape[0] // (RING * RING)
    for i in range(RING):
        for j in range(RING):
            total = 0.0
            for s in range(RING):
                where = ((i - s) % RING, j) if major else (i, (j - s) % RING)
                at = (where[0] * RING + where[1]) * slot
                total = total + factors[first_scalar + s] * came[s][at : at + slot].astype(
                    jnp.float32
                )
            at = (i * RING + j) * slot
            out[at : at + slot] = total.astype(jnp.bfloat16)


def down_rows(held, loaded, loaded_other, at, span, outs):
    units = loaded.shape[0]
    group = held.shape[0] // RING
    block = min(span, 512)
    for start in range(0, span, block):
        where = slice(at + start, at + start + block)
        product = dot(held[:, :units], loaded[:, where]) + dot(
            held[:, units:], loaded_other[:, where]
        )
        product = product.astype(jnp.bfloat16)
        for n, out in enumerate(outs):
            out[:, start : start + block] = product[n * group : (n + 1) * group]


def combine(parts, scalars, first_scalar, major):
    rows, width = parts[0].shape

    def kernel(*refs):
        came = dict(zip(ORDER, refs[:RING]))
        turn_rows(came, refs[RING], first_scalar, major, refs[RING + 1])

    return call(
        kernel,
        "combine",
        0,
        10 * rows * width,
        [*parts, scalars],
        [jax.ShapeDtypeStruct((rows, width), jnp.bfloat16)],
        [VMEM] * RING + [SCALARS],
    )[0]


def combine_down(parts, scalars, first_scalar, major, weights, at, span):
    rows, width = parts[0].shape

    def kernel(*refs):
        came = dict(zip(ORDER, refs[:RING]))
        factors, loaded, loaded_other, value, *outs = refs[RING:]
        turn_rows(came, factors, first_scalar, major, value)
        down_rows(value, loaded, loaded_other, at, span, outs)

    value, *outs = call(
        kernel,
        "combine_down",
        2 * rows * width * span,
        2 * width * span,
        [*parts, scalars, *weights],
        [jax.ShapeDtypeStruct((rows, width), jnp.bfloat16)]
        + [jax.ShapeDtypeStruct((rows // RING, span), jnp.bfloat16)] * RING,
        [VMEM] * RING + [SCALARS] + [VMEM] * 2,
    )
    return value, outs


def down(value, weights, at, span):
    rows, width = value.shape

    def kernel(held, loaded, loaded_other, *outs):
        down_rows(held, loaded, loaded_other, at, span, outs)

    return call(
        kernel,
        "down",
        2 * rows * width * span,
        2 * width * span,
        [value, *weights],
        [jax.ShapeDtypeStruct((rows // RING, span), jnp.bfloat16)] * RING,
    )


def fold(sides):
    count = len(sides[0])
    group = sides[0][0].shape[0]
    rows = group // RING
    width = sum(parts[0].shape[1] for parts in sides)

    def kernel(*refs):
        ins, outs = refs[: count * len(sides)], refs[count * len(sides) :]
        start = 0
        for n in range(len(sides)):
            parts = ins[count * n : count * (n + 1)]
            stop = start + parts[0].shape[1]
            for m, out in enumerate(outs):
                at = slice(m * rows, (m + 1) * rows)
                total = sum(part[at].astype(jnp.float32) for part in parts)
                out[:, start:stop] = total.astype(jnp.bfloat16)
            start = stop

    return call(
        kernel,
        "fold",
        0,
        10 * group * width,
        [part for parts in sides for part in parts],
        [jax.ShapeDtypeStruct((rows, width), jnp.bfloat16)] * RING,
    )


def to_steps(parts, along):
    return parts[0], send(parts[2], along(2)), send(parts[1], along(1)), send(parts[3], along(-1))


def body(tokens, gate_weight, up_weight, down_weight, mixing):
    width = tokens.shape[1]
    index = lax.axis_index("tensor")
    scalars = lax.dynamic_index_in_dim(jnp.asarray(scalar_table()), index, keepdims=False)

    gate, up = gate_weight.T, up_weight.T
    cuts = cuts_of(GATHER_SPANS, width)
    others = send(gate, SIBLING), send(up, SIBLING)

    near = from_steps(tokens, along_first, TOKEN_ORDER)
    (own,) = load((tokens,), 0, width)
    own = after(own, scalars)
    blocks = stack((own, *near), cuts)
    value = None
    for n, (at, span) in enumerate(cuts):
        pieces = (blocks[n], *from_steps(blocks[n], along_second, ORDER))
        finish = (mixing, scalars) if n == len(cuts) - 1 else None
        if n == 0:
            value = gate_up(pieces, (), (gate, up, *others), at, span, value, finish)
        else:
            close = load((after(gate, value), up), at, span)
            value = gate_up(pieces, close, others, at, span, value, finish)

    down_own = after(down_weight, value)
    down_other = send(down_own, SIBLING)
    value = combine((value, *from_steps(value, along_first, ORDER)), scalars, 1, False)
    left, right = cuts_of(OUT_SPANS, width)
    weights = (down_own, down_other)
    parts = (value, *from_steps(value, along_second, ORDER))
    value, partial = combine_down(parts, scalars, 1 + RING, True, weights, *left)
    sides = [to_steps(partial, along_second)]
    sides.append(to_steps(down(value, weights, *right), along_second))
    parts = to_steps(fold(sides), along_first)
    return sum(part.astype(jnp.float32) for part in parts).astype(jnp.bfloat16)


def solution(mesh):
    in_specs = (
        P(("dp", "tensor"), None),
        P(None, "tensor"),
        P(None, "tensor"),
        P("tensor", None),
        P(),
    )
    out_specs = P(("dp", "tensor"), None)
    return jax.shard_map(body, mesh=mesh, in_specs=in_specs, out_specs=out_specs, check_vma=False)
```

```python
import math

import jax
import jax.numpy as jnp
import numpy as np
from jax import lax
from jax.experimental import pallas as pl
from jax.experimental.pallas import tpu as pltpu
from jax.sharding import PartitionSpec as P

RING = 4
TOKEN_ORDER = (0, 2, 1, 3)
ORDER = (0, 1, 3, 2)
PLACES = [(x, y, c) for x in range(RING) for y in range(RING) for c in range(2)]
GATHER_SPANS = (1, 1)
OUT_SPANS = (3, 5)
LIMIT = 24 * 2**20
SMALL = 16 * 2**20
BY_ROWS = (((1,), (1,)), ((), ()))


def place(x, y, c):
    return (x % RING) * RING * 2 + (y % RING) * 2 + c


def along_first(d):
    return [
        (place(x, y, c), place(x + d, y, c) if c == 0 else place(x, y + d, c))
        for x, y, c in PLACES
    ]


def along_second(d):
    return [
        (place(x, y, c), place(x + d, y, c) if c == 1 else place(x, y + d, c))
        for x, y, c in PLACES
    ]


SIBLING = [(place(x, y, c), place(x, y, 1 - c)) for x, y, c in PLACES]


def send(value, pairs):
    return lax.ppermute(value, "tensor", pairs)


def from_steps(value, along, order):
    return [send(value, along({1: -1, 2: 2, 3: 1}[step])) for step in order[1:]]


def after(value, *others):
    return lax.optimization_barrier((value, *others))[0]


def dot(a, b):
    return jnp.dot(a, b, preferred_element_type=jnp.float32)


def scalar_table():
    def sign(row, column):
        return 1.0 - 2.0 * (bin(row & column).count("1") % 2)

    rows = []
    for x, y, c in PLACES:
        first, second = (x, y) if c == 0 else (y, x)
        row = [1.0 - 2.0 * c]
        row += [sign(first, (first + s) % RING) for s in range(RING)]
        row += [
            sign(second, (second + s) % RING) / math.sqrt(2 * RING * RING) for s in range(RING)
        ]
        rows.append(row + [0.0] * (16 - len(row)))
    return np.array(rows, np.float32)


def cuts_of(shares, total):
    widths = [w * total // sum(shares) for w in shares]
    starts = [sum(widths[:n]) for n in range(len(widths))]
    return list(zip(starts, widths))


VMEM = pl.BlockSpec(memory_space=pltpu.VMEM)
SCALARS = pl.BlockSpec(memory_space=pltpu.SMEM)


def call(kernel, name, flops, size, operands, outs, specs=None, limit=SMALL, **kwargs):
    return pl.pallas_call(
        kernel,
        name=name,
        compiler_params=pltpu.CompilerParams(vmem_limit_bytes=limit),
        cost_estimate=pl.CostEstimate(flops=flops, bytes_accessed=size, transcendentals=0),
        in_specs=specs or [VMEM] * len(operands),
        out_specs=[VMEM] * len(outs),
        out_shape=outs,
        **kwargs,
    )(*operands)


def in_hbm(value):
    return pltpu.with_memory_space_constraint(value, pltpu.HBM)


def load(values, at, span):
    count = len(values)

    def kernel(*refs):
        sems = refs[-1]
        copies = [
            pltpu.make_async_copy(refs[n].at[:, pl.ds(at, span)], refs[count + n], sems.at[n])
            for n in range(count)
        ]
        for copy in copies:
            copy.start()
        for copy in copies:
            copy.wait()

    return pl.pallas_call(
        kernel,
        name="load",
        compiler_params=pltpu.CompilerParams(vmem_limit_bytes=SMALL),
        cost_estimate=pl.CostEstimate(
            flops=0,
            bytes_accessed=sum(4 * value.shape[0] * span for value in values),
            transcendentals=0,
        ),
        in_specs=[pl.BlockSpec(memory_space=pltpu.HBM)] * count,
        out_specs=[VMEM] * count,
        out_shape=[pltpu.VMEM((value.shape[0], span), value.dtype) for value in values],
        scratch_shapes=[pltpu.SemaphoreType.DMA((count,))],
    )(*[in_hbm(value) for value in values])


def stack(parts, cuts):
    rows = parts[0].shape[0]

    def kernel(*refs):
        ins, outs = refs[: len(parts)], refs[len(parts) :]
        for (at, span), out in zip(cuts, outs):
            for n, part in zip(TOKEN_ORDER, ins):
                out[n * rows : (n + 1) * rows] = part[:, at : at + span]

    return call(
        kernel,
        "stack",
        0,
        sum(4 * rows * len(parts) * span for _, span in cuts),
        parts,
        [jax.ShapeDtypeStruct((rows * len(parts), span), jnp.bfloat16) for _, span in cuts],
    )


def local(gate, up, mixing):
    hidden = (gate / (1.0 + jnp.exp(-gate)) * up).astype(jnp.bfloat16)
    return dot(hidden, mixing[...])


def gate_up(pieces, close, weights, at, span, sums, finish):
    group = pieces[0].shape[0]
    rows = RING * group
    units = weights[0].shape[0]
    block = math.gcd(span, 4096)
    steps = span // block
    opening, closing = sums is None, finish is not None
    count = len(close)

    def kernel(*refs):
        refs = list(refs)
        parts, near = refs[:RING], refs[RING : RING + count]
        far = refs[RING + count : RING + 4]
        refs = refs[RING + 4 :]
        x, held, sems, refs = refs[-3], refs[-2], refs[-1], refs[:-3]
        before = None if opening else refs.pop(0)
        if closing:
            mixing, scalars, out, total = refs
        else:
            (total,) = refs
        copies = [
            [
                pltpu.make_async_copy(
                    load.at[:, pl.ds(at + step * block, block)], held.at[step, n], sems.at[step, n]
                )
                for step in range(steps)
            ]
            for n, load in enumerate(far)
        ]
        for step in range(steps):
            for n in range(4 - count):
                copies[n][step].start()
        for n, part in zip(ORDER, parts):
            x[n * group : (n + 1) * group] = part[...]
        for n in range(count):
            product = lax.dot_general(
                x[...], near[n][...], BY_ROWS, preferred_element_type=jnp.float32
            )
            total[n] = product if opening else before[n] + product
        if closing and count == 2:
            own = local(total[0], total[1], mixing)
        for step in range(steps):
            here = x[:, step * block : (step + 1) * block]
            for n in range(4 - count):
                copies[n][step].wait()
                product = lax.dot_general(
                    here, held[step, n], BY_ROWS, preferred_element_type=jnp.float32
                )
                if step > 0:
                    total[count + n] += product
                else:
                    total[count + n] = product if opening else before[count + n] + product
        if closing:
            if count != 2:
                own = local(total[0], total[1], mixing)
            other = local(total[2], total[3], mixing)
            turn = scalars[0]
            out[:, :units] = (other + turn * own).astype(jnp.bfloat16)
            out[:, units:] = (own - turn * other).astype(jnp.bfloat16)

    operands = [*pieces, *close, *[in_hbm(w) for w in weights]]
    specs = [VMEM] * (RING + count) + [pl.BlockSpec(memory_space=pltpu.HBM)] * (4 - count)
    scratch = [
        pltpu.VMEM((rows, span), jnp.bfloat16),
        pltpu.VMEM((steps, 4 - count, units, block), jnp.bfloat16),
        pltpu.SemaphoreType.DMA((steps, 4 - count)),
    ]
    if not opening:
        operands.append(sums)
        specs.append(VMEM)
    if closing:
        operands += finish
        specs += [VMEM, SCALARS]
        out = jax.ShapeDtypeStruct((rows, 2 * units), jnp.bfloat16)
        scratch = [pltpu.VMEM((4, rows, units), jnp.float32)] + scratch
    else:
        out = jax.ShapeDtypeStruct((4, rows, units), jnp.float32)
    return call(
        kernel,
        "gate_up",
        8 * rows * units * span,
        8 * units * span,
        operands,
        [out],
        specs,
        LIMIT if opening else SMALL,
        scratch_shapes=scratch,
    )[0]


def turn_rows(came, factors, first_scalar, major, out):
    slot = out.shape[0] // (RING * RING)
    for i in range(RING):
        for j in range(RING):
            total = 0.0
            for s in range(RING):
                where = ((i - s) % RING, j) if major else (i, (j - s) % RING)
                at = (where[0] * RING + where[1]) * slot
                total = total + factors[first_scalar + s] * came[s][at : at + slot].astype(
                    jnp.float32
                )
            at = (i * RING + j) * slot
            out[at : at + slot] = total.astype(jnp.bfloat16)


def down_rows(held, loaded, loaded_other, at, span, outs):
    units = loaded.shape[0]
    group = held.shape[0] // RING
    block = min(span, 512)
    for start in range(0, span, block):
        where = slice(at + start, at + start + block)
        product = dot(held[:, :units], loaded[:, where]) + dot(
            held[:, units:], loaded_other[:, where]
        )
        product = product.astype(jnp.bfloat16)
        for n, out in enumerate(outs):
            out[:, start : start + block] = product[n * group : (n + 1) * group]


def combine(parts, scalars, first_scalar, major):
    rows, width = parts[0].shape

    def kernel(*refs):
        came = dict(zip(ORDER, refs[:RING]))
        turn_rows(came, refs[RING], first_scalar, major, refs[RING + 1])

    return call(
        kernel,
        "combine",
        0,
        10 * rows * width,
        [*parts, scalars],
        [jax.ShapeDtypeStruct((rows, width), jnp.bfloat16)],
        [VMEM] * RING + [SCALARS],
    )[0]


def combine_down(parts, scalars, first_scalar, major, weights, at, span):
    rows, width = parts[0].shape

    def kernel(*refs):
        came = dict(zip(ORDER, refs[:RING]))
        factors, loaded, loaded_other, value, *outs = refs[RING:]
        turn_rows(came, factors, first_scalar, major, value)
        down_rows(value, loaded, loaded_other, at, span, outs)

    value, *outs = call(
        kernel,
        "combine_down",
        2 * rows * width * span,
        2 * width * span,
        [*parts, scalars, *weights],
        [jax.ShapeDtypeStruct((rows, width), jnp.bfloat16)]
        + [jax.ShapeDtypeStruct((rows // RING, span), jnp.bfloat16)] * RING,
        [VMEM] * RING + [SCALARS] + [VMEM] * 2,
    )
    return value, outs


def down(value, weights, at, span):
    rows, width = value.shape

    def kernel(held, loaded, loaded_other, *outs):
        down_rows(held, loaded, loaded_other, at, span, outs)

    return call(
        kernel,
        "down",
        2 * rows * width * span,
        2 * width * span,
        [value, *weights],
        [jax.ShapeDtypeStruct((rows // RING, span), jnp.bfloat16)] * RING,
    )


def fold(sides):
    count = len(sides[0])
    group = sides[0][0].shape[0]
    rows = group // RING
    width = sum(parts[0].shape[1] for parts in sides)

    def kernel(*refs):
        ins, outs = refs[: count * len(sides)], refs[count * len(sides) :]
        start = 0
        for n in range(len(sides)):
            parts = ins[count * n : count * (n + 1)]
            stop = start + parts[0].shape[1]
            for m, out in enumerate(outs):
                at = slice(m * rows, (m + 1) * rows)
                total = sum(part[at].astype(jnp.float32) for part in parts)
                out[:, start:stop] = total.astype(jnp.bfloat16)
            start = stop

    return call(
        kernel,
        "fold",
        0,
        10 * group * width,
        [part for parts in sides for part in parts],
        [jax.ShapeDtypeStruct((rows, width), jnp.bfloat16)] * RING,
    )


def to_steps(parts, along):
    return parts[0], send(parts[2], along(2)), send(parts[1], along(1)), send(parts[3], along(-1))


def body(tokens, gate_weight, up_weight, down_weight, mixing):
    width = tokens.shape[1]
    index = lax.axis_index("tensor")
    scalars = lax.dynamic_index_in_dim(jnp.asarray(scalar_table()), index, keepdims=False)

    gate, up = gate_weight.T, up_weight.T
    cuts = cuts_of(GATHER_SPANS, width)
    others = send(gate, SIBLING), send(up, SIBLING)

    near = from_steps(tokens, along_first, TOKEN_ORDER)
    (own,) = load((tokens,), 0, width)
    own = after(own, scalars)
    blocks = stack((own, *near), cuts)
    value = None
    for n, (at, span) in enumerate(cuts):
        pieces = (blocks[n], *from_steps(blocks[n], along_second, ORDER))
        finish = (mixing, scalars) if n == len(cuts) - 1 else None
        if n == 0:
            value = gate_up(pieces, (), (gate, up, *others), at, span, value, finish)
        else:
            close = load((after(gate, value), up), at, span)
            value = gate_up(pieces, close, others, at, span, value, finish)

    down_own = after(down_weight, value)
    down_other = send(down_own, SIBLING)
    value = combine((value, *from_steps(value, along_first, ORDER)), scalars, 1, False)
    left, right = cuts_of(OUT_SPANS, width)
    weights = (down_own, down_other)
    parts = (value, *from_steps(value, along_second, ORDER))
    value, partial = combine_down(parts, scalars, 1 + RING, True, weights, *left)
    sides = [to_steps(partial, along_second)]
    sides.append(to_steps(down(value, weights, *right), along_second))
    parts = to_steps(fold(sides), along_first)
    return sum(part.astype(jnp.float32) for part in parts).astype(jnp.bfloat16)


def solution(mesh):
    in_specs = (
        P(("dp", "tensor"), None),
        P(None, "tensor"),
        P(None, "tensor"),
        P("tensor", None),
        P(),
    )
    out_specs = P(("dp", "tensor"), None)
    return jax.shard_map(body, mesh=mesh, in_specs=in_specs, out_specs=out_specs, check_vma=False)
```
